32 devices in a mesh: groups: 2 (over x), rows: 16 (over z, y, core).
Axes of the slice: x: 2, y: 2, z: 4, core: 2. Of those that a mesh axis runs over, the one named last changes fastest.
Arguments:
- features: bfloat16 [128, 4, 3072], P(('groups', 'rows')), parts along dimension 0, may hold values from -6 to 6
- cotangent: bfloat16 [128, 4, 3072], P(('groups', 'rows')), parts along dimension 0, may hold values from -6 to 6
- depth_kernel: float32 [7, 7, 3072], replicated, may hold values from -0.875 to 0.875
- depth_bias: float32 [3072], replicated, may hold values from -3 to 3
- norm_gain: float32 [3072], replicated, may hold values from 0.1 to 1.9
- norm_shift: float32 [3072], replicated, may hold values from -3 to 3
- up_weight: bfloat16 [3072, 12288], P(None, 'rows'), may hold values from -0.109375 to 0.109375
- up_bias: float32 [12288], P('rows'), may hold values from -3 to 3
- down_weight: bfloat16 [12288, 3072], P('rows'), may hold values from -0.109375 to 0.109375
- layer_scale: float32 [3072], replicated, may hold values from 0.3 to 3
Outputs:
- input_grad: bfloat16 [128, 4, 3072], P(('groups', 'rows')), parts along dimension 0
- up_grad: float32 [6144, 12288], P('groups', 'rows'), parts along dimension 0
- up_bias_grad: float32 [24576], P(('groups', 'rows')), parts along dimension 0
- down_grad: float32 [24576, 3072], P(('groups', 'rows')), parts along dimension 0
- kernel_grad: float32 [14, 7, 3072], P('groups'), parts along dimension 0
- depth_bias_grad: float32 [6144], P('groups'), parts along dimension 0
- gain_grad: float32 [6144], P('groups'), parts along dimension 0
- shift_grad: float32 [6144], P('groups'), parts along dimension 0
The draws below stay inside these ranges and needn't reach their ends.
There are 2 independent parts, one for each index of `groups`. The reference program is written for one: setup_inputs(seed, part) draws one part's arguments, and reference() takes and returns one part's arrays. A program takes and returns all parts, laid end to end along the dimension named above; an argument that names none is the same for every part. Nothing has to cross between parts.
All inputs are finite; a program needn't handle non-finite values.
Results may differ from the reference program's by a relative error of at most 0.0075.
Values may be sent and summed in bfloat16 or wider, within the bound.
No kernel may reach another device: no remote copies, remote signals or barrier semaphores. Data moves between devices by JAX's collectives and lax.ppermute only.
A program may use at most 128 MiB of HBM per device.

```python
import math
import jax
import jax.numpy as jnp
from jax import lax

D = 3072
FF = 12288
COLS = 4
IMG_ROWS = 32
ROWS = 64
TOKENS = 256


def shard_levels(rng, dims, pieces, smallest, high):
    loudness = 1.0
    for axis_at, blocks in pieces:
        draws = jax.random.uniform(jax.random.fold_in(jax.random.fold_in(rng, 6), axis_at), (blocks,), jnp.float32, smallest / len(pieces), high / len(pieces))
        loudness = loudness * jnp.repeat(jnp.exp(draws), dims[axis_at] // blocks).reshape((-1,) + (1,) * (len(dims) - 1 - axis_at))
    return loudness


def noise(key, dims, width, bound, cuts=(), kind=jnp.bfloat16):
    values = width * jax.random.normal(key, dims, jnp.float32)
    if cuts:
        values = values * shard_levels(key, dims, cuts, -0.22, 0.18)
    return jnp.clip(values, -bound, bound).astype(kind)


def setup_inputs(seed: int = 0, part: int = 0) -> dict:
    keys = jax.random.split(jax.random.key(seed), 11)
    part_splits = jax.random.split(jax.random.fold_in(keys[10], part), 11)
    features = noise(part_splits[0], (ROWS, COLS, D), 1.0, 6.0, ((0, 16),))
    cotangent = noise(part_splits[1], (ROWS, COLS, D), 1.0, 6.0, ((0, 16),))
    depth_kernel = noise(keys[2], (7, 7, D), 49 ** -0.5, 0.875, (), jnp.float32)
    depth_bias = noise(keys[3], (D,), 0.5, 3.0, (), jnp.float32)
    norm_gain = jnp.clip(1.0 + 0.18 * jax.random.normal(keys[4], (D,), jnp.float32), 0.1, 1.9)
    norm_shift = noise(keys[5], (D,), 0.5, 3.0, (), jnp.float32)
    up_weight = noise(keys[6], (D, FF), D ** -0.5, 0.109375, ((1, 16),))
    up_bias = noise(keys[7], (FF,), 0.5, 3.0, ((0, 16),), jnp.float32)
    down_weight = noise(keys[8], (FF, D), D ** -0.5, 0.109375, ((0, 16),))
    layer_scale = jnp.clip(jnp.exp(jax.random.uniform(keys[9], (D,), jnp.float32, math.log(0.3), math.log(3.0))), 0.3, 3.0)
    return {"features": features, "cotangent": cotangent, "depth_kernel": depth_kernel, "depth_bias": depth_bias, "norm_gain": norm_gain, "norm_shift": norm_shift, "up_weight": up_weight, "up_bias": up_bias, "down_weight": down_weight, "layer_scale": layer_scale}


def gelu_value(pre_act):
    return 0.5 * pre_act * (1.0 + jax.scipy.special.erf(pre_act * 0.7071067811865476))

def gelu_slope(pre_act):
    cdf_part = 0.5 * (1.0 + jax.scipy.special.erf(pre_act * 0.7071067811865476))
    return cdf_part + pre_act * jnp.exp(-0.5 * pre_act * pre_act) * 0.3989422804014327

def contract(left, right, left_dim, right_dim):
    return lax.dot_general(left, right, (((left_dim,), (right_dim,)), ((), ())), preferred_element_type=jnp.float32)

def depthwise(padded, kernel, offset_term, row_count, col_count):
    summed = jnp.zeros(padded[..., 3:3 + row_count, 3:3 + col_count, :].shape, padded.dtype)
    for tap_row in range(7):
        for tap_col in range(7):
            summed = summed + kernel[tap_row, tap_col] * padded[..., tap_row:tap_row + row_count, tap_col:tap_col + col_count, :]
    return summed + offset_term

def depthwise_back(padded_grad, kernel, row_count, col_count):
    summed = jnp.zeros(padded_grad[..., 3:3 + row_count, 3:3 + col_count, :].shape, padded_grad.dtype)
    for tap_row in range(7):
        for tap_col in range(7):
            summed = summed + kernel[tap_row, tap_col] * padded_grad[..., 6 - tap_row:6 - tap_row + row_count, 6 - tap_col:6 - tap_col + col_count, :]
    return summed

def normalize(conv_out):
    row_mean = lax.optimization_barrier(jnp.mean(conv_out, axis=-1, keepdims=True))
    centred = conv_out - row_mean
    inv_std = lax.rsqrt(lax.optimization_barrier(jnp.mean(centred * centred, axis=-1, keepdims=True)) + 1e-06)
    return (centred * inv_std, inv_std)

def norm_back(norm_grad, unit_norm, inv_std, norm_gain):
    scaled = norm_grad * norm_gain
    return inv_std * (scaled - lax.optimization_barrier(jnp.mean(scaled, axis=-1, keepdims=True)) - unit_norm * lax.optimization_barrier(jnp.mean(scaled * unit_norm, axis=-1, keepdims=True)))

def reference(features, cotangent, depth_kernel, depth_bias, norm_gain, norm_shift, up_weight, up_bias, down_weight, layer_scale):
    images = ROWS // IMG_ROWS
    half_image = IMG_ROWS // 2
    rolled_in = jnp.roll(features, -half_image, axis=0)
    rolled_cot = jnp.roll(cotangent, -half_image, axis=0)
    stacked = rolled_in.astype(jnp.float32).reshape(images, IMG_ROWS, COLS, D)
    padded = jnp.pad(stacked, ((0, 0), (3, 3), (3, 3), (0, 0)))
    conv_out = depthwise(padded, depth_kernel, depth_bias, IMG_ROWS, COLS)
    unit_norm, inv_std = normalize(conv_out)
    normed = (unit_norm * norm_gain + norm_shift).astype(jnp.bfloat16).reshape(TOKENS, D)
    pre_act = jnp.dot(normed, up_weight, preferred_element_type=jnp.float32) + up_bias
    hidden = gelu_value(pre_act).astype(jnp.bfloat16)
    cot_scaled = (rolled_cot.astype(jnp.float32) * layer_scale).astype(jnp.bfloat16).reshape(TOKENS, D)
    down_grad = contract(hidden, cot_scaled, 0, 0)
    hid_grad = contract(cot_scaled, down_weight, 1, 1)
    act_grad = (hid_grad * gelu_slope(pre_act)).astype(jnp.bfloat16)
    up_bias_grad = lax.optimization_barrier(jnp.sum(act_grad.astype(jnp.float32), axis=0))
    up_grad = contract(normed, act_grad, 0, 0)
    norm_grad = contract(act_grad, up_weight, 1, 1).reshape(images, IMG_ROWS, COLS, D)
    gain_grad = lax.optimization_barrier(jnp.sum(norm_grad * unit_norm, axis=(0, 1, 2)))
    shift_grad = lax.optimization_barrier(jnp.sum(norm_grad, axis=(0, 1, 2)))
    conv_grad = norm_back(norm_grad, unit_norm, inv_std, norm_gain)
    depth_bias_grad = lax.optimization_barrier(jnp.sum(conv_grad, axis=(0, 1, 2)))
    kernel_rows = []
    for tap_row in range(7):
        kernel_cols = []
        for tap_col in range(7):
            kernel_cols.append(lax.optimization_barrier(jnp.sum(conv_grad * padded[:, tap_row:tap_row + IMG_ROWS, tap_col:tap_col + COLS, :], axis=(0, 1, 2))))
        kernel_rows.append(jnp.stack(kernel_cols))
    kernel_grad = jnp.stack(kernel_rows)
    grad_padded = jnp.pad(conv_grad, ((0, 0), (3, 3), (3, 3), (0, 0)))
    back_term = depthwise_back(grad_padded, depth_kernel, IMG_ROWS, COLS).reshape(ROWS, COLS, D)
    back_term = jnp.roll(back_term, half_image, axis=0)
    input_grad = (cotangent.astype(jnp.float32) + back_term).astype(jnp.bfloat16)
    return (input_grad, up_grad, up_bias_grad, down_grad, kernel_grad, depth_bias_grad, gain_grad, shift_grad)
```

```python
import jax
import jax.numpy as jnp
from jax import lax
from jax.sharding import PartitionSpec as P

IMG_ROWS = 32
BF16 = jnp.bfloat16
F32 = jnp.float32


def stages_of(count):
    sizes = []
    chips = count // 2
    while chips % 4 == 0 and chips > 4:
        sizes.append(4)
        chips //= 4
    if chips > 1:
        sizes.append(chips)
    out = [(1, 2)]
    stride = 2
    for size in reversed(sizes):
        out.insert(0, (stride, size))
        stride *= size
    return out


def from_ahead(count, stride, size, step):
    pairs = []
    for i in range(count):
        digit = (i // stride) % size
        src = i + ((digit + step) % size - digit) * stride
        pairs.append((src, i))
    return pairs


def send(value, pairs):
    return lax.ppermute(value, "rows", pairs)


def gather_stage(value, count, stride, size):
    parts = [value]
    for step in range(1, size):
        parts.append(send(value, from_ahead(count, stride, size, step)))
    return jnp.stack(parts)


def scatter_stage(value, count, stride, size):
    total = value[0].astype(F32)
    for step in range(1, size):
        back = [(dst, src) for src, dst in from_ahead(count, stride, size, step)]
        total = total + send(value[step], back).astype(F32)
    return total


def gelu_parts(pre_act):
    cdf = 0.5 * (1.0 + jax.scipy.special.erf(pre_act * 0.7071067811865476))
    slope = cdf + pre_act * jnp.exp(-0.5 * pre_act * pre_act) * 0.3989422804014327
    return pre_act * cdf, slope


def contract(left, right, left_dim, right_dim):
    return lax.dot_general(
        left, right, (((left_dim,), (right_dim,)), ((), ())), preferred_element_type=F32
    )


def extended(cells, width, fwd, bwd):
    head = lax.slice_in_dim(cells, 0, width, axis=0)
    tail = lax.slice_in_dim(cells, cells.shape[0] - width, cells.shape[0], axis=0)
    return jnp.concatenate([send(tail, fwd), cells, send(head, bwd)], axis=0)


def on_device(
    features,
    cotangent,
    depth_kernel,
    depth_bias,
    norm_gain,
    norm_shift,
    up_weight,
    up_bias,
    down_weight,
    layer_scale,
):
    rows_dev, cols, channels = features.shape
    count = lax.axis_size("rows")
    stages = stages_of(count)
    shard = rows_dev * cols
    half_image = IMG_ROWS // 2
    crossing = [
        (i, (i + 1) % count)
        for i in range(count)
        if ((i + 1) * rows_dev - half_image) % IMG_ROWS != 0
    ]
    fwd = crossing
    bwd = [(b, a) for a, b in crossing]
    pieces = 2
    width = channels // pieces

    def gather(value):
        outs = []
        for p in range(pieces):
            part = value[:, p * width : (p + 1) * width]
            for stride, size in stages:
                part = gather_stage(part, count, stride, size)
            outs.append(part.reshape(shard * count, width))
        return outs

    near = extended(features, 3, fwd, bwd).astype(F32)
    cot_scaled = (
        (cotangent.astype(F32) * layer_scale).astype(BF16).reshape(shard, channels)
    )
    cot_all = gather(cot_scaled)
    padded = jnp.pad(near, ((0, 0), (3, 3), (0, 0)))
    conv_out = jnp.zeros((rows_dev, cols, channels), F32)
    for i in range(7):
        for j in range(7):
            conv_out = conv_out + depth_kernel[i, j] * padded[i : i + rows_dev, j : j + cols]
    conv_out = conv_out + depth_bias
    row_mean = jnp.mean(conv_out, axis=-1, keepdims=True)
    centred = conv_out - row_mean
    inv_std = lax.rsqrt(jnp.mean(centred * centred, axis=-1, keepdims=True) + 1e-06)
    unit_norm = centred * inv_std
    normed = (unit_norm * norm_gain + norm_shift).astype(BF16).reshape(shard, channels)
    normed_all = gather(normed)

    hid_grad = sum(
        contract(cot_all[p], down_weight[:, p * width : (p + 1) * width], 1, 1)
        for p in range(pieces)
    )
    pre_act = up_bias + sum(
        contract(normed_all[p], up_weight[p * width : (p + 1) * width], 1, 0)
        for p in range(pieces)
    )
    value, slope = gelu_parts(pre_act)
    hidden = value.astype(BF16)
    act_grad = (hid_grad * slope).astype(BF16)

    norm_parts = []
    for p in range(pieces):
        part = contract(act_grad, up_weight[p * width : (p + 1) * width], 1, 1).astype(BF16)
        lead = [size for _, size in reversed(stages)]
        part = part.reshape(*lead, shard, width)
        for stride, size in reversed(stages):
            part = scatter_stage(part, count, stride, size)
            if stride != stages[0][0]:
                part = part.astype(BF16)
        norm_parts.append(part)
    norm_grad = jnp.concatenate(norm_parts, axis=-1).reshape(rows_dev, cols, channels)

    up_bias_grad = jnp.sum(act_grad.astype(F32), axis=0)
    down_grad = jnp.concatenate([contract(hidden, c, 0, 0) for c in cot_all], axis=1)
    up_grad = jnp.concatenate([contract(n, act_grad, 0, 0) for n in normed_all], axis=0)

    gain_part = jnp.sum(norm_grad * unit_norm, axis=(0, 1))
    shift_part = jnp.sum(norm_grad, axis=(0, 1))
    scaled = norm_grad * norm_gain
    conv_grad = inv_std * (
        scaled
        - jnp.mean(scaled, axis=-1, keepdims=True)
        - unit_norm * jnp.mean(scaled * unit_norm, axis=-1, keepdims=True)
    )
    bias_part = jnp.sum(conv_grad, axis=(0, 1))
    rows_out = [
        jnp.sum(conv_grad * padded[i : i + rows_dev, j : j + cols], axis=(0, 1))
        for i in range(7)
        for j in range(7)
    ]
    near_grad = extended(conv_grad.astype(BF16), 3, fwd, bwd).astype(F32)
    grad_padded = jnp.pad(near_grad, ((0, 0), (3, 3), (0, 0)))

    chips = count // 2
    per = -(-52 // chips)
    small = jnp.stack(rows_out + [gain_part, shift_part, bias_part])
    small = jnp.pad(small, ((0, per * chips - 52), (0, 0)))
    half = channels // 2
    small = small.reshape(chips, per, 2, half).transpose(2, 0, 1, 3)
    core = lax.axis_index("rows") % 2
    swapped = jnp.where(core == 0, small, small[::-1])
    swapped = swapped.astype(BF16)
    mine = swapped[0].astype(F32) + send(
        swapped[1], from_ahead(count, 1, 2, 1)
    ).astype(F32)
    mine = mine.astype(BF16)
    chip = lax.axis_index("rows") // 2
    ahead = jnp.roll(mine, -chip, axis=0)
    total = ahead[0].astype(F32)
    for step in range(1, chips):
        back = [(dst, src) for src, dst in from_ahead(count, 2, chips, step)]
        total = total + send(ahead[step], back).astype(F32)
    total = total.astype(BF16)
    every = [total] + [
        send(total, from_ahead(count, 2, chips, step)) for step in range(1, chips)
    ]
    every = jnp.roll(jnp.stack(every), chip, axis=0)
    other = send(every, from_ahead(count, 1, 2, 1))
    both = jnp.where(
        core == 0,
        jnp.concatenate([every, other], axis=-1),
        jnp.concatenate([other, every], axis=-1),
    )
    both = both.reshape(per * chips, channels).astype(F32)
    kernel_grad = both[:49].reshape(7, 7, channels)
    gain_grad, shift_grad, depth_bias_grad = both[49], both[50], both[51]

    back_term = jnp.zeros((rows_dev, cols, channels), F32)
    for i in range(7):
        for j in range(7):
            back_term = back_term + depth_kernel[i, j] * grad_padded[
                6 - i : 6 - i + rows_dev, 6 - j : 6 - j + cols
            ]
    input_grad = (cotangent.astype(F32) + back_term).astype(BF16)
    return (
        input_grad,
        up_grad,
        up_bias_grad,
        down_grad,
        kernel_grad,
        depth_bias_grad,
        gain_grad,
        shift_grad,
    )


def solution(mesh):
    in_specs = (
        P(("groups", "rows"), None, None),
        P(("groups", "rows"), None, None),
        P(),
        P(),
        P(),
        P(),
        P(None, "rows"),
        P("rows"),
        P("rows", None),
        P(),
    )
    out_specs = (
        P(("groups", "rows"), None, None),
        P("groups", "rows"),
        P(("groups", "rows")),
        P(("groups", "rows"), None),
        P("groups", None, None),
        P("groups"),
        P("groups"),
        P("groups"),
    )
    return jax.shard_map(
        on_device, mesh=mesh, in_specs=in_specs, out_specs=out_specs, check_vma=False
    )
```

```python
import jax
import jax.numpy as jnp
from jax import lax
from jax.experimental import pallas as pl
from jax.experimental.pallas import tpu as pltpu
from jax.sharding import PartitionSpec as P

IMG_ROWS = 32
BF16 = jnp.bfloat16
F32 = jnp.float32


def stages_of(count):
    sizes = []
    chips = count // 2
    while chips % 4 == 0 and chips > 4:
        sizes.append(4)
        chips //= 4
    if chips > 1:
        sizes.append(chips)
    out = [(1, 2)]
    stride = 2
    for size in reversed(sizes):
        out.insert(0, (stride, size))
        stride *= size
    return out


def from_ahead(count, stride, size, step):
    pairs = []
    for i in range(count):
        digit = (i // stride) % size
        src = i + ((digit + step) % size - digit) * stride
        pairs.append((src, i))
    return pairs


def send(value, pairs):
    return lax.ppermute(value, "rows", pairs)


def gather_stage(value, count, stride, size):
    parts = [value]
    for step in range(1, size):
        parts.append(send(value, from_ahead(count, stride, size, step)))
    return jnp.stack(parts)


def scatter_stage(value, count, stride, size):
    total = value[0].astype(F32)
    for step in range(1, size):
        back = [(dst, src) for src, dst in from_ahead(count, stride, size, step)]
        total = total + send(value[step], back).astype(F32)
    return total


def gelu_parts(pre_act):
    cdf = 0.5 * (1.0 + jax.scipy.special.erf(pre_act * 0.7071067811865476))
    slope = cdf + pre_act * jnp.exp(-0.5 * pre_act * pre_act) * 0.3989422804014327
    return pre_act * cdf, slope


def contract(left, right, left_dim, right_dim):
    return lax.dot_general(
        left, right, (((left_dim,), (right_dim,)), ((), ())), preferred_element_type=F32
    )


def extended(cells, width, fwd, bwd):
    head = lax.slice_in_dim(cells, 0, width, axis=0)
    tail = lax.slice_in_dim(cells, cells.shape[0] - width, cells.shape[0], axis=0)
    return jnp.concatenate([send(tail, fwd), cells, send(head, bwd)], axis=0)


def generic_device(
    features,
    cotangent,
    depth_kernel,
    depth_bias,
    norm_gain,
    norm_shift,
    up_weight,
    up_bias,
    down_weight,
    layer_scale,
):
    rows_dev, cols, channels = features.shape
    count = lax.axis_size("rows")
    stages = stages_of(count)
    shard = rows_dev * cols
    half_image = IMG_ROWS // 2
    crossing = [
        (i, (i + 1) % count)
        for i in range(count)
        if ((i + 1) * rows_dev - half_image) % IMG_ROWS != 0
    ]
    fwd = crossing
    bwd = [(b, a) for a, b in crossing]
    pieces = 2
    width = channels // pieces

    def gather(value):
        outs = []
        for p in range(pieces):
            part = value[:, p * width : (p + 1) * width]
            for stride, size in stages:
                part = gather_stage(part, count, stride, size)
            outs.append(part.reshape(shard * count, width))
        return outs

    near = extended(features, 3, fwd, bwd).astype(F32)
    cot_scaled = (
        (cotangent.astype(F32) * layer_scale).astype(BF16).reshape(shard, channels)
    )
    cot_all = gather(cot_scaled)
    padded = jnp.pad(near, ((0, 0), (3, 3), (0, 0)))
    conv_out = jnp.zeros((rows_dev, cols, channels), F32)
    for i in range(7):
        for j in range(7):
            conv_out = conv_out + depth_kernel[i, j] * padded[i : i + rows_dev, j : j + cols]
    conv_out = conv_out + depth_bias
    row_mean = jnp.mean(conv_out, axis=-1, keepdims=True)
    centred = conv_out - row_mean
    inv_std = lax.rsqrt(jnp.mean(centred * centred, axis=-1, keepdims=True) + 1e-06)
    unit_norm = centred * inv_std
    normed = (unit_norm * norm_gain + norm_shift).astype(BF16).reshape(shard, channels)
    normed_all = gather(normed)

    hid_grad = sum(
        contract(cot_all[p], down_weight[:, p * width : (p + 1) * width], 1, 1)
        for p in range(pieces)
    )
    pre_act = up_bias + sum(
        contract(normed_all[p], up_weight[p * width : (p + 1) * width], 1, 0)
        for p in range(pieces)
    )
    value, slope = gelu_parts(pre_act)
    hidden = value.astype(BF16)
    act_grad = (hid_grad * slope).astype(BF16)

    norm_parts = []
    for p in range(pieces):
        part = contract(act_grad, up_weight[p * width : (p + 1) * width], 1, 1).astype(BF16)
        lead = [size for _, size in reversed(stages)]
        part = part.reshape(*lead, shard, width)
        for stride, size in reversed(stages):
            part = scatter_stage(part, count, stride, size)
            if stride != stages[0][0]:
                part = part.astype(BF16)
        norm_parts.append(part)
    norm_grad = jnp.concatenate(norm_parts, axis=-1).reshape(rows_dev, cols, channels)

    up_bias_grad = jnp.sum(act_grad.astype(F32), axis=0)
    down_grad = jnp.concatenate([contract(hidden, c, 0, 0) for c in cot_all], axis=1)
    up_grad = jnp.concatenate([contract(n, act_grad, 0, 0) for n in normed_all], axis=0)

    gain_part = jnp.sum(norm_grad * unit_norm, axis=(0, 1))
    shift_part = jnp.sum(norm_grad, axis=(0, 1))
    scaled = norm_grad * norm_gain
    conv_grad = inv_std * (
        scaled
        - jnp.mean(scaled, axis=-1, keepdims=True)
        - unit_norm * jnp.mean(scaled * unit_norm, axis=-1, keepdims=True)
    )
    bias_part = jnp.sum(conv_grad, axis=(0, 1))
    rows_out = [
        jnp.sum(conv_grad * padded[i : i + rows_dev, j : j + cols], axis=(0, 1))
        for i in range(7)
        for j in range(7)
    ]
    near_grad = extended(conv_grad.astype(BF16), 3, fwd, bwd).astype(F32)
    grad_padded = jnp.pad(near_grad, ((0, 0), (3, 3), (0, 0)))

    chips = count // 2
    per = -(-52 // chips)
    small = jnp.stack(rows_out + [gain_part, shift_part, bias_part])
    small = jnp.pad(small, ((0, per * chips - 52), (0, 0)))
    half = channels // 2
    small = small.reshape(chips, per, 2, half).transpose(2, 0, 1, 3)
    core = lax.axis_index("rows") % 2
    swapped = jnp.where(core == 0, small, small[::-1])
    swapped = swapped.astype(BF16)
    mine = swapped[0].astype(F32) + send(
        swapped[1], from_ahead(count, 1, 2, 1)
    ).astype(F32)
    mine = mine.astype(BF16)
    chip = lax.axis_index("rows") // 2
    ahead = jnp.roll(mine, -chip, axis=0)
    total = ahead[0].astype(F32)
    for step in range(1, chips):
        back = [(dst, src) for src, dst in from_ahead(count, 2, chips, step)]
        total = total + send(ahead[step], back).astype(F32)
    total = total.astype(BF16)
    every = [total] + [
        send(total, from_ahead(count, 2, chips, step)) for step in range(1, chips)
    ]
    every = jnp.roll(jnp.stack(every), chip, axis=0)
    other = send(every, from_ahead(count, 1, 2, 1))
    both = jnp.where(
        core == 0,
        jnp.concatenate([every, other], axis=-1),
        jnp.concatenate([other, every], axis=-1),
    )
    both = both.reshape(per * chips, channels).astype(F32)
    kernel_grad = both[:49].reshape(7, 7, channels)
    gain_grad, shift_grad, depth_bias_grad = both[49], both[50], both[51]

    back_term = jnp.zeros((rows_dev, cols, channels), F32)
    for i in range(7):
        for j in range(7):
            back_term = back_term + depth_kernel[i, j] * grad_padded[
                6 - i : 6 - i + rows_dev, 6 - j : 6 - j + cols
            ]
    input_grad = (cotangent.astype(F32) + back_term).astype(BF16)
    return (
        input_grad,
        up_grad,
        up_bias_grad,
        down_grad,
        kernel_grad,
        depth_bias_grad,
        gain_grad,
        shift_grad,
    )


LANES = 128
VMEM = pltpu.VMEM
VSPEC = pl.BlockSpec(memory_space=pltpu.VMEM)
SSPEC = pl.BlockSpec(memory_space=pltpu.SMEM)
PARAMS = pltpu.CompilerParams(vmem_limit_bytes=40 * 1024 * 1024)
GRID_PARAMS = pltpu.CompilerParams(
    vmem_limit_bytes=40 * 1024 * 1024, dimension_semantics=("arbitrary",)
)
EXACT = lax.Precision.HIGHEST


def z_pairs(step):
    return from_ahead(16, 4, 4, step)


Y_PAIRS = from_ahead(16, 2, 2, 1)
C_PAIRS = from_ahead(16, 1, 2, 1)


def gather_tokens(shard):
    planes = [shard] + [send(shard, z_pairs(step)) for step in (1, 2, 3)]
    across = [send(plane, Y_PAIRS) for plane in planes]
    core_planes = send(jnp.stack(planes), C_PAIRS)
    core_across = send(jnp.stack(across), C_PAIRS)
    return (*planes, *across, core_planes, core_across)


def each_piece(idx, pieces):
    z, y, c = idx[0], idx[1], idx[2]
    for yr in range(2):
        for cr in range(2):
            for step in range(4):
                if cr == 0:
                    piece = pieces[4 * yr + step]
                else:
                    piece = pieces[8 + yr].at[step]
                place = (z + step + 3) % 4
                image = place // 2
                row = 16 * (place % 2) + 8 * ((y + yr) % 2) + 4 * ((c + cr) % 2)
                yield piece, image, row


def lane_tile(tile):
    return pl.ds(pl.multiple_of(tile * LANES, LANES), LANES)


def conv_norm_kernel(idx, *refs):
    pieces = refs[:10]
    kern, bias, gain, shift = refs[10:14]
    normed, f_slice, u_slice, inv_slice = refs[14:18]
    feats, conv, total, mean_ref, inv_ref = refs[18:]
    tiles = feats.shape[0]
    edge = jnp.zeros((tiles, 8, 8, LANES), F32)
    feats[:, :, 0:8, :] = edge
    feats[:, :, 40:48, :] = edge
    for piece, image, row in each_piece(idx, pieces):
        for tile in range(tiles):
            block = piece[:, tile * LANES : (tile + 1) * LANES].astype(F32)
            for col in range(4):
                feats[tile, image * 4 + col, pl.ds(8 + row, 4), :] = block[
                    4 * col : 4 * col + 4
                ]
    total[...] = jnp.zeros_like(total)

    def conv_tile(tile, carry):
        lanes = lane_tile(tile)
        for image in range(2):
            for part in range(2):
                acc = [jnp.broadcast_to(bias[0:1, lanes], (16, LANES))] * 4
                for i in range(7):
                    for src in range(4):
                        rows = feats[tile, image * 4 + src, pl.ds(5 + 16 * part + i, 16), :]
                        for col in range(4):
                            j = src - col + 3
                            acc[col] = acc[col] + kern[i, j : j + 1, lanes] * rows
                for col in range(4):
                    at = pl.ds(image * 128 + col * 32 + 16 * part, 16)
                    conv[tile, at, :] = acc[col]
                    total[at, :] = total[at, :] + acc[col]
        return carry

    lax.fori_loop(0, tiles, conv_tile, 0)
    channels = tiles * LANES
    mean = jnp.sum(total[...], axis=-1, keepdims=True) / channels
    mean_ref[...] = jnp.broadcast_to(mean, mean_ref.shape)
    total[...] = jnp.zeros_like(total)

    def square_tile(tile, carry):
        centred = conv[tile] - mean_ref[...]
        total[...] = total[...] + centred * centred
        return carry

    lax.fori_loop(0, tiles, square_tile, 0)
    spread = jnp.sum(total[...], axis=-1, keepdims=True) / channels
    inv_ref[...] = jnp.broadcast_to(lax.rsqrt(spread + 1e-06), inv_ref.shape)
    place = lax.broadcasted_iota(jnp.int32, (16, LANES), 0)

    def norm_tile(tile, carry):
        lanes = lane_tile(tile)
        scale, offset = gain[0:1, lanes], shift[0:1, lanes]
        unit = (conv[tile] - mean_ref[...]) * inv_ref[...]
        normed[pl.ds(0, 256), lanes] = (unit * scale + offset).astype(BF16)
        scale_hi = scale.astype(BF16).astype(F32)
        offset_hi = offset.astype(BF16).astype(F32)
        extra = jnp.where(place == 0, scale_hi, 0.0)
        extra = jnp.where(place == 1, scale - scale_hi, extra)
        extra = jnp.where(place == 2, offset_hi, extra)
        extra = jnp.where(place == 3, offset - offset_hi, extra)
        normed[pl.ds(256, 16), lanes] = extra.astype(BF16)
        return carry

    lax.fori_loop(0, tiles, norm_tile, 0)
    chip, core = idx[0] * 2 + idx[1], idx[2]
    own = pl.ds(pl.multiple_of(core * 128, 128), 128)
    inv_slice[...] = inv_ref[own, :]
    for k in range(3):
        tile = chip * 3 + k
        u_slice[k] = (conv[tile, own, :] - mean_ref[own, :]) * inv_ref[own, :]
        for col in range(4):
            f_slice[k, col] = feats[tile, core * 4 + col]


def cot_kernel(idx, *refs):
    pieces = refs[:10]
    layer_scale, cot_all, cot_slice, raw = refs[10:]
    tiles = cot_all.shape[1] // LANES
    for piece, image, row in each_piece(idx, pieces):
        for tile in range(tiles):
            block = piece[:, tile * LANES : (tile + 1) * LANES].astype(F32)
            for col in range(4):
                raw[tile, pl.ds(image * 128 + col * 32 + row, 4), :] = block[
                    4 * col : 4 * col + 4
                ]
    for tile in range(tiles):
        lanes = slice(tile * LANES, (tile + 1) * LANES)
        cot_all[:, lanes] = (raw[tile] * layer_scale[0:1, lanes]).astype(BF16)
    chip, core = idx[0] * 2 + idx[1], idx[2]
    for k in range(3):
        cot_slice[k] = raw[chip * 3 + k, pl.ds(pl.multiple_of(core * 128, 128), 128), :]


def up_kernel(normed, weight, up_bias, hidden, slope, centred, gain_dot):
    product = jnp.dot(normed[...], weight[...], preferred_element_type=F32)
    plain = product[0:256]
    pre_act = plain + up_bias[0:1, :]
    cdf = 0.5 * (1.0 + lax.erf(pre_act * 0.7071067811865476))
    hidden[...] = (pre_act * cdf).astype(BF16)
    slope[...] = cdf + pre_act * jnp.exp(-0.5 * pre_act * pre_act) * 0.3989422804014327
    centred[...] = plain - (product[258:259] + product[259:260])
    gain_dot[...] = jnp.broadcast_to(product[256:257] + product[257:258], gain_dot.shape)


def act_kernel(cot_all, weight, slope, centred, gain_dot, act_grad, bias_grad, sums, first, second):
    hid_grad = contract(cot_all[...], weight[...], 1, 1)
    act = (hid_grad * slope[...]).astype(BF16)
    act_grad[...] = act
    act = act.astype(F32)
    bias_grad[...] = jnp.broadcast_to(jnp.sum(act, axis=0, keepdims=True), bias_grad.shape)

    @pl.when(pl.program_id(0) == 0)
    def _():
        first[...] = jnp.zeros_like(first)
        second[...] = jnp.zeros_like(second)

    for tile in range(act.shape[1] // LANES):
        lanes = slice(tile * LANES, (tile + 1) * LANES)
        first[...] = first[...] + act[:, lanes] * gain_dot[0:1, lanes]
        second[...] = second[...] + act[:, lanes] * centred[:, lanes]

    @pl.when(pl.program_id(0) == pl.num_programs(0) - 1)
    def _():
        ones = jnp.ones((8, LANES), F32)
        for image in range(2):
            at = slice(image * 128, (image + 1) * 128)
            for row, ref in ((0, first), (8, second)):
                sums[image, row : row + 8, :] = lax.dot_general(
                    ones, ref[at, :], (((1,), (1,)), ((), ())),
                    precision=EXACT, preferred_element_type=F32,
                )


def norm_grad_kernel(idx, act_grad, weight, sums, keep, away):
    core = idx[2]
    for ref, image in ((keep, core), (away, 1 - core)):
        at = pl.ds(pl.multiple_of(image * 128, 128), 128)
        ref[0, 0:128, :] = contract(act_grad[at, :], weight[...], 1, 1).astype(ref.dtype)
        ref[0, 128:144, 0:128] = sums[image].astype(ref.dtype)
        ref[0, 128:144, 128:384] = jnp.zeros((16, 256), ref.dtype)


def conv_back_kernel(
    idx, own, near_1, near_2, near_3, f_slice, u_slice, inv_slice, gain, kern, cot_slice,
    ig_keep, core_msg, small_keep, cg, back, small,
):
    chip, y, core = idx[0] * 2 + idx[1], idx[1], idx[2]
    channels = gain.shape[1]

    def summed(rows, lanes):
        return (
            own[rows, lanes]
            + near_1[rows, lanes].astype(F32)
            + near_2[rows, lanes].astype(F32)
            + near_3[rows, lanes].astype(F32)
        )

    sums = summed(slice(128, 144), slice(0, 128))
    place = lax.broadcasted_iota(jnp.int32, (16, LANES), 0)

    def per_token(row):
        pick = jnp.where(place == row, 1.0 / channels, 0.0).astype(F32)
        return lax.dot_general(
            sums, pick, (((0,), (0,)), ((), ())), precision=EXACT, preferred_element_type=F32
        )

    mean_1, mean_2 = per_token(0), per_token(8)
    cg[:, :, 0:8, :] = jnp.zeros((3, 4, 8, LANES), F32)
    cg[:, :, 40:48, :] = jnp.zeros((3, 4, 8, LANES), F32)
    small[...] = jnp.zeros_like(small)
    for k in range(3):
        lanes = slice(k * LANES, (k + 1) * LANES)
        wide = lane_tile(chip * 3 + k)
        norm_grad = summed(slice(0, 128), lanes)
        unit = u_slice[k]
        scaled = norm_grad * gain[0:1, wide]
        grad = inv_slice[...] * (scaled - mean_1 - unit * mean_2)
        for col in range(4):
            cg[k, col, 8:40, :] = grad[32 * col : 32 * col + 32]
        small[56:57, lanes] = jnp.sum(norm_grad * unit, axis=0, keepdims=True)
        small[57:58, lanes] = jnp.sum(norm_grad, axis=0, keepdims=True)
        small[58:59, lanes] = jnp.sum(grad, axis=0, keepdims=True)
        for i in range(7):
            acc = [None] * 7
            for src in range(4):
                rows = f_slice[k, src, 5 + i : 37 + i, :]
                for col in range(4):
                    j = src - col + 3
                    term = cg[k, col, 8:40, :] * rows
                    acc[j] = term if acc[j] is None else acc[j] + term
            for j in range(7):
                small[8 * i + j : 8 * i + j + 1, lanes] = jnp.sum(acc[j], axis=0, keepdims=True)
        for part in range(2):
            acc = [
                cot_slice[k, 32 * col + 16 * part : 32 * col + 16 * part + 16, :]
                for col in range(4)
            ]
            for i in range(7):
                for src in range(4):
                    start = 11 + 16 * part - i
                    rows = cg[k, src, start : start + 16, :]
                    for col in range(4):
                        j = col - src + 3
                        acc[col] = acc[col] + kern[i, j : j + 1, wide] * rows
            for col in range(4):
                back[k, col, 16 * part : 16 * part + 16, :] = acc[col]
        for half in range(2):
            for yr in range(2):
                for cr in range(2):
                    start = 16 * half + 8 * ((y + yr) % 2) + 4 * ((core + cr) % 2)
                    block = jnp.concatenate(
                        [back[k, col, pl.ds(start, 4), :] for col in range(4)], axis=0
                    )
                    ref = core_msg if cr else ig_keep
                    ref[2 * half + yr, :, lanes] = block.astype(BF16)
    for part in range(2):
        away = pl.ds(pl.multiple_of(32 * (1 - core) + 16 * part, 16), 16)
        core_msg[4 + part] = small[away, :].astype(BF16)
        mine = pl.ds(pl.multiple_of(32 * core + 16 * part, 16), 16)
        small_keep[part] = small[mine, :]


def route_kernel(idx, ig_keep, core_msg, small_keep, *msgs):
    z, core = idx[0], idx[2]
    total = [
        (small_keep[part] + core_msg[4 + part].astype(F32)).astype(BF16) for part in range(2)
    ]
    for step in range(4):
        place = (z + step + 3) % 4
        image, half = place // 2, place % 2
        for yr in range(2):
            kept, came = ig_keep[2 * half + yr], core_msg[2 * half + yr]
            msgs[step][yr] = jnp.where(image == core, kept, came)
        for part in range(2):
            msgs[step][2 + part] = total[part]


def place_kernel(idx, *refs):
    msgs, came, core_a, core_b = refs[:4], refs[4], refs[5], refs[6]
    tokens, small = refs[7], refs[8]
    z, y, core = idx[0], idx[1], idx[2]
    for step in range(4):
        plane = (z + 4 - step) % 4
        for yr in range(2):
            chip = plane * 2 + (y + yr) % 2
            lanes = pl.ds(pl.multiple_of(chip * 384, 128), 384)
            tokens[:, lanes] = came[step, 0] if yr else msgs[step][0]
            for part in range(2):
                mine = came[step, 1 + part] if yr else msgs[step][2 + part]
                other = core_b[step, part] if yr else core_a[step, part]
                for block, at in ((mine, core), (other, 1 - core)):
                    block = block.astype(F32)
                    for sub in range(2):
                        small[4 * at + 2 * part + sub, :, lanes] = block[8 * sub : 8 * sub + 8]


def call(kernel, out_shape, inputs, specs, scratch=()):
    return pl.pallas_call(
        kernel,
        out_shape=out_shape,
        in_specs=specs,
        out_specs=jax.tree.map(lambda _: VSPEC, out_shape),
        scratch_shapes=list(scratch),
        compiler_params=PARAMS,
    )(*inputs)


def shape(dims, dtype):
    return jax.ShapeDtypeStruct(dims, dtype)


def sliced_device(
    features,
    cotangent,
    depth_kernel,
    depth_bias,
    norm_gain,
    norm_shift,
    up_weight,
    up_bias,
    down_weight,
    layer_scale,
):
    channels, hidden_dev = up_weight.shape
    tiles = channels // LANES
    index = lax.axis_index("rows")
    idx = jnp.stack([index // 4, (index // 2) % 2, index % 2]).astype(jnp.int32)
    bias_row, gain_row = depth_bias.reshape(1, channels), norm_gain.reshape(1, channels)
    shift_row, scale_row = norm_shift.reshape(1, channels), layer_scale.reshape(1, channels)

    feat_shard = features.transpose(1, 0, 2).reshape(16, channels)
    cot_shard = cotangent.transpose(1, 0, 2).reshape(16, channels)
    feat_pieces = gather_tokens(feat_shard)
    cot_pieces = gather_tokens(cot_shard)

    normed, f_slice, u_slice, inv_slice = call(
        conv_norm_kernel,
        (
            shape((272, channels), BF16),
            shape((3, 4, 48, LANES), F32),
            shape((3, 128, LANES), F32),
            shape((128, LANES), F32),
        ),
        (idx, *feat_pieces, depth_kernel, bias_row, gain_row, shift_row),
        [SSPEC] + [VSPEC] * 14,
        (
            VMEM((tiles, 8, 48, LANES), F32),
            VMEM((tiles, 256, LANES), F32),
            VMEM((256, LANES), F32),
            VMEM((256, LANES), F32),
            VMEM((256, LANES), F32),
        ),
    )
    cot_all, cot_slice = call(
        cot_kernel,
        (shape((256, channels), BF16), shape((3, 128, LANES), F32)),
        (idx, *cot_pieces, scale_row),
        [SSPEC] + [VSPEC] * 11,
        (VMEM((tiles, 256, LANES), F32),),
    )

    tile = 256
    steps = hidden_dev // tile
    hidden, slope, centred, gain_dot = pl.pallas_call(
        up_kernel,
        grid=(steps,),
        out_shape=(
            shape((256, hidden_dev), BF16),
            shape((256, hidden_dev), F32),
            shape((256, hidden_dev), F32),
            shape((8, hidden_dev), F32),
        ),
        in_specs=[
            pl.BlockSpec((272, channels), lambda n: (0, 0)),
            pl.BlockSpec((channels, tile), lambda n: (0, n)),
            pl.BlockSpec((1, tile), lambda n: (0, n)),
        ],
        out_specs=(
            pl.BlockSpec((256, tile), lambda n: (0, n)),
            pl.BlockSpec((256, tile), lambda n: (0, n)),
            pl.BlockSpec((256, tile), lambda n: (0, n)),
            pl.BlockSpec((8, tile), lambda n: (0, n)),
        ),
        compiler_params=GRID_PARAMS,
    )(normed, up_weight, up_bias.reshape(1, hidden_dev))

    act_grad, bias_grad, sums = pl.pallas_call(
        act_kernel,
        grid=(steps,),
        out_shape=(
            shape((256, hidden_dev), BF16),
            shape((8, hidden_dev), F32),
            shape((2, 16, LANES), F32),
        ),
        in_specs=[
            pl.BlockSpec((256, channels), lambda n: (0, 0)),
            pl.BlockSpec((tile, channels), lambda n: (n, 0)),
            pl.BlockSpec((256, tile), lambda n: (0, n)),
            pl.BlockSpec((256, tile), lambda n: (0, n)),
            pl.BlockSpec((8, tile), lambda n: (0, n)),
        ],
        out_specs=(
            pl.BlockSpec((256, tile), lambda n: (0, n)),
            pl.BlockSpec((8, tile), lambda n: (0, n)),
            pl.BlockSpec((2, 16, LANES), lambda n: (0, 0, 0)),
        ),
        scratch_shapes=[VMEM((256, LANES), F32), VMEM((256, LANES), F32)],
        compiler_params=GRID_PARAMS,
    )(cot_all, down_weight, slope, centred, gain_dot)

    def norm_grad_for(step):
        def weight_block(yr, idx):
            return (2 * ((idx[0] + step) % 4) + (idx[1] + yr) % 2, 0)

        return pl.pallas_call(
            norm_grad_kernel,
            grid_spec=pltpu.PrefetchScalarGridSpec(
                num_scalar_prefetch=1,
                grid=(2,),
                in_specs=[
                    pl.BlockSpec((256, hidden_dev), lambda yr, idx: (0, 0)),
                    pl.BlockSpec((384, hidden_dev), weight_block),
                    pl.BlockSpec((2, 16, LANES), lambda yr, idx: (0, 0, 0)),
                ],
                out_specs=(
                    pl.BlockSpec((1, 144, 384), lambda yr, idx: (yr, 0, 0)),
                    pl.BlockSpec((1, 144, 384), lambda yr, idx: (yr, 0, 0)),
                ),
            ),
            out_shape=(shape((2, 144, 384), F32), shape((2, 144, 384), BF16)),
            compiler_params=GRID_PARAMS,
        )(idx, act_grad, up_weight, sums)

    arrived = {}
    for step in (1, 2, 3, 0):
        keep, away = norm_grad_for(step)
        came = send(away, C_PAIRS)
        across = send((keep[1] + came[1].astype(F32)).astype(BF16), Y_PAIRS)
        total = keep[0] + came[0].astype(F32) + across.astype(F32)
        if step:
            back = [(dst, src) for src, dst in z_pairs(step)]
            total = send(total.astype(BF16), back)
        arrived[step] = total

    ig_keep, core_msg, small_keep = call(
        conv_back_kernel,
        (shape((4, 16, 384), BF16), shape((6, 16, 384), BF16), shape((2, 16, 384), F32)),
        (
            idx, arrived[0], arrived[1], arrived[2], arrived[3], f_slice, u_slice, inv_slice,
            gain_row, depth_kernel, cot_slice,
        ),
        [SSPEC] + [VSPEC] * 10,
        (
            VMEM((3, 4, 48, LANES), F32),
            VMEM((3, 4, 32, LANES), F32),
            VMEM((64, 384), F32),
        ),
    )
    core_msg = send(core_msg, C_PAIRS)
    msgs = call(
        route_kernel,
        tuple(shape((4, 16, 384), BF16) for _ in range(4)),
        (idx, ig_keep, core_msg, small_keep),
        [SSPEC] + [VSPEC] * 3,
    )
    msgs = [msgs[0]] + [
        send(msgs[step], [(dst, src) for src, dst in z_pairs(step)]) for step in (1, 2, 3)
    ]
    came = send(jnp.stack([msg[1:4] for msg in msgs]), Y_PAIRS)
    core_a = send(jnp.stack([msg[2:4] for msg in msgs]), C_PAIRS)
    core_b = send(came[:, 1:3], C_PAIRS)
    tokens, small = call(
        place_kernel,
        (shape((16, channels), BF16), shape((8, 8, channels), F32)),
        (idx, *msgs, came, core_a, core_b),
        [SSPEC] + [VSPEC] * 7,
    )
    down_grad = contract(hidden, cot_all, 0, 0)
    up_grad = contract(normed[0:256], act_grad, 0, 0)
    return (
        tokens.reshape(4, 4, channels).transpose(1, 0, 2),
        up_grad,
        bias_grad[0],
        down_grad,
        small[0:7, 0:7],
        small[7, 2],
        small[7, 0],
        small[7, 1],
    )


def on_device(features, *rest):
    rows_dev, cols, channels = features.shape
    fits = lax.axis_size("rows") == 16 and rows_dev == 4 and cols == 4 and channels == 3072
    return (sliced_device if fits else generic_device)(features, *rest)


def solution(mesh):
    in_specs = (
        P(("groups", "rows"), None, None),
        P(("groups", "rows"), None, None),
        P(),
        P(),
        P(),
        P(),
        P(None, "rows"),
        P("rows"),
        P("rows", None),
        P(),
    )
    out_specs = (
        P(("groups", "rows"), None, None),
        P("groups", "rows"),
        P(("groups", "rows")),
        P(("groups", "rows"), None),
        P("groups", None, None),
        P("groups"),
        P("groups"),
        P("groups"),
    )
    return jax.shard_map(
        on_device, mesh=mesh, in_specs=in_specs, out_specs=out_specs, check_vma=False
    )
```

```python
import functools

import jax
import jax.numpy as jnp
from jax import lax
from jax.experimental import pallas as pl
from jax.experimental.pallas import tpu as pltpu
from jax.sharding import PartitionSpec as P

IMG_ROWS = 32
BF16 = jnp.bfloat16
F32 = jnp.float32


def stages_of(count):
    sizes = []
    chips = count // 2
    while chips % 4 == 0 and chips > 4:
        sizes.append(4)
        chips //= 4
    if chips > 1:
        sizes.append(chips)
    out = [(1, 2)]
    stride = 2
    for size in reversed(sizes):
        out.insert(0, (stride, size))
        stride *= size
    return out


def from_ahead(count, stride, size, step):
    pairs = []
    for i in range(count):
        digit = (i // stride) % size
        src = i + ((digit + step) % size - digit) * stride
        pairs.append((src, i))
    return pairs


def send(value, pairs):
    return lax.ppermute(value, "rows", pairs)


def gather_stage(value, count, stride, size):
    parts = [value]
    for step in range(1, size):
        parts.append(send(value, from_ahead(count, stride, size, step)))
    return jnp.stack(parts)


def scatter_stage(value, count, stride, size):
    total = value[0].astype(F32)
    for step in range(1, size):
        back = [(dst, src) for src, dst in from_ahead(count, stride, size, step)]
        total = total + send(value[step], back).astype(F32)
    return total


def gelu_parts(pre_act):
    cdf = 0.5 * (1.0 + jax.scipy.special.erf(pre_act * 0.7071067811865476))
    slope = cdf + pre_act * jnp.exp(-0.5 * pre_act * pre_act) * 0.3989422804014327
    return pre_act * cdf, slope


def contract(left, right, left_dim, right_dim):
    return lax.dot_general(
        left, right, (((left_dim,), (right_dim,)), ((), ())), preferred_element_type=F32
    )


def extended(cells, width, fwd, bwd):
    head = lax.slice_in_dim(cells, 0, width, axis=0)
    tail = lax.slice_in_dim(cells, cells.shape[0] - width, cells.shape[0], axis=0)
    return jnp.concatenate([send(tail, fwd), cells, send(head, bwd)], axis=0)


def generic_device(
    features,
    cotangent,
    depth_kernel,
    depth_bias,
    norm_gain,
    norm_shift,
    up_weight,
    up_bias,
    down_weight,
    layer_scale,
):
    rows_dev, cols, channels = features.shape
    count = lax.axis_size("rows")
    stages = stages_of(count)
    shard = rows_dev * cols
    half_image = IMG_ROWS // 2
    crossing = [
        (i, (i + 1) % count)
        for i in range(count)
        if ((i + 1) * rows_dev - half_image) % IMG_ROWS != 0
    ]
    fwd = crossing
    bwd = [(b, a) for a, b in crossing]
    pieces = 2
    width = channels // pieces

    def gather(value):
        outs = []
        for p in range(pieces):
            part = value[:, p * width : (p + 1) * width]
            for stride, size in stages:
                part = gather_stage(part, count, stride, size)
            outs.append(part.reshape(shard * count, width))
        return outs

    near = extended(features, 3, fwd, bwd).astype(F32)
    cot_scaled = (
        (cotangent.astype(F32) * layer_scale).astype(BF16).reshape(shard, channels)
    )
    cot_all = gather(cot_scaled)
    padded = jnp.pad(near, ((0, 0), (3, 3), (0, 0)))
    conv_out = jnp.zeros((rows_dev, cols, channels), F32)
    for i in range(7):
        for j in range(7):
            conv_out = conv_out + depth_kernel[i, j] * padded[i : i + rows_dev, j : j + cols]
    conv_out = conv_out + depth_bias
    row_mean = jnp.mean(conv_out, axis=-1, keepdims=True)
    centred = conv_out - row_mean
    inv_std = lax.rsqrt(jnp.mean(centred * centred, axis=-1, keepdims=True) + 1e-06)
    unit_norm = centred * inv_std
    normed = (unit_norm * norm_gain + norm_shift).astype(BF16).reshape(shard, channels)
    normed_all = gather(normed)

    hid_grad = sum(
        contract(cot_all[p], down_weight[:, p * width : (p + 1) * width], 1, 1)
        for p in range(pieces)
    )
    pre_act = up_bias + sum(
        contract(normed_all[p], up_weight[p * width : (p + 1) * width], 1, 0)
        for p in range(pieces)
    )
    value, slope = gelu_parts(pre_act)
    hidden = value.astype(BF16)
    act_grad = (hid_grad * slope).astype(BF16)

    norm_parts = []
    for p in range(pieces):
        part = contract(act_grad, up_weight[p * width : (p + 1) * width], 1, 1).astype(BF16)
        lead = [size for _, size in reversed(stages)]
        part = part.reshape(*lead, shard, width)
        for stride, size in reversed(stages):
            part = scatter_stage(part, count, stride, size)
            if stride != stages[0][0]:
                part = part.astype(BF16)
        norm_parts.append(part)
    norm_grad = jnp.concatenate(norm_parts, axis=-1).reshape(rows_dev, cols, channels)

    up_bias_grad = jnp.sum(act_grad.astype(F32), axis=0)
    down_grad = jnp.concatenate([contract(hidden, c, 0, 0) for c in cot_all], axis=1)
    up_grad = jnp.concatenate([contract(n, act_grad, 0, 0) for n in normed_all], axis=0)

    gain_part = jnp.sum(norm_grad * unit_norm, axis=(0, 1))
    shift_part = jnp.sum(norm_grad, axis=(0, 1))
    scaled = norm_grad * norm_gain
    conv_grad = inv_std * (
        scaled
        - jnp.mean(scaled, axis=-1, keepdims=True)
        - unit_norm * jnp.mean(scaled * unit_norm, axis=-1, keepdims=True)
    )
    bias_part = jnp.sum(conv_grad, axis=(0, 1))
    rows_out = [
        jnp.sum(conv_grad * padded[i : i + rows_dev, j : j + cols], axis=(0, 1))
        for i in range(7)
        for j in range(7)
    ]
    near_grad = extended(conv_grad.astype(BF16), 3, fwd, bwd).astype(F32)
    grad_padded = jnp.pad(near_grad, ((0, 0), (3, 3), (0, 0)))

    chips = count // 2
    per = -(-52 // chips)
    small = jnp.stack(rows_out + [gain_part, shift_part, bias_part])
    small = jnp.pad(small, ((0, per * chips - 52), (0, 0)))
    half = channels // 2
    small = small.reshape(chips, per, 2, half).transpose(2, 0, 1, 3)
    core = lax.axis_index("rows") % 2
    swapped = jnp.where(core == 0, small, small[::-1])
    swapped = swapped.astype(BF16)
    mine = swapped[0].astype(F32) + send(
        swapped[1], from_ahead(count, 1, 2, 1)
    ).astype(F32)
    mine = mine.astype(BF16)
    chip = lax.axis_index("rows") // 2
    ahead = jnp.roll(mine, -chip, axis=0)
    total = ahead[0].astype(F32)
    for step in range(1, chips):
        back = [(dst, src) for src, dst in from_ahead(count, 2, chips, step)]
        total = total + send(ahead[step], back).astype(F32)
    total = total.astype(BF16)
    every = [total] + [
        send(total, from_ahead(count, 2, chips, step)) for step in range(1, chips)
    ]
    every = jnp.roll(jnp.stack(every), chip, axis=0)
    other = send(every, from_ahead(count, 1, 2, 1))
    both = jnp.where(
        core == 0,
        jnp.concatenate([every, other], axis=-1),
        jnp.concatenate([other, every], axis=-1),
    )
    both = both.reshape(per * chips, channels).astype(F32)
    kernel_grad = both[:49].reshape(7, 7, channels)
    gain_grad, shift_grad, depth_bias_grad = both[49], both[50], both[51]

    back_term = jnp.zeros((rows_dev, cols, channels), F32)
    for i in range(7):
        for j in range(7):
            back_term = back_term + depth_kernel[i, j] * grad_padded[
                6 - i : 6 - i + rows_dev, 6 - j : 6 - j + cols
            ]
    input_grad = (cotangent.astype(F32) + back_term).astype(BF16)
    return (
        input_grad,
        up_grad,
        up_bias_grad,
        down_grad,
        kernel_grad,
        depth_bias_grad,
        gain_grad,
        shift_grad,
    )


LANES = 128
VMEM = pltpu.VMEM
VSPEC = pl.BlockSpec(memory_space=pltpu.VMEM)
SSPEC = pl.BlockSpec(memory_space=pltpu.SMEM)
EXACT = lax.Precision.HIGHEST
MIB = 1024 * 1024


def z_pairs(step):
    return from_ahead(16, 4, 4, step)


def flipped(pairs):
    return [(dst, src) for src, dst in pairs]


Y_PAIRS = from_ahead(16, 2, 2, 1)
C_PAIRS = from_ahead(16, 1, 2, 1)


def after(value, other):
    return lax.optimization_barrier((value, other))[0]


def gather_chips(shard):
    with jax.named_scope("feat_z"):
        planes = [shard] + [send(shard, z_pairs(step)) for step in (1, 2, 3)]
    with jax.named_scope("feat_y"):
        return planes, [send(plane, Y_PAIRS) for plane in planes]


def lane_tile(tile):
    return pl.ds(pl.multiple_of(tile * LANES, LANES), LANES)


def sixteen(block):
    return pl.ds(pl.multiple_of(block * 16, 16), 16)


def place_and_convolve(idx, pieces, came, kern, bias, feats, conv, turn, total, first_tile):
    z, y, core = idx[0], idx[1], idx[2]
    tiles = feats.shape[0]
    edge = jnp.zeros((tiles, 4, 8, LANES), F32)
    feats[:, :, 0:8, :] = edge
    feats[:, :, 40:48, :] = edge

    def place(piece, row):
        for tile in range(tiles):
            lanes = slice((first_tile + tile) * LANES, (first_tile + tile + 1) * LANES)
            for r in range(4):
                turn[tile % 4, 4 * r : 4 * r + 4, :] = piece[r, :, lanes].astype(F32)
            for col in range(4):
                feats[tile, col, pl.ds(8 + row, 4), :] = turn[
                    tile % 4, pl.ds(col, 4, stride=4), :
                ]

    for yr in range(2):
        for step in range(4):
            at = (z + step + 3) % 4

            @pl.when(at // 2 == core)
            def _():
                place(pieces[4 * yr + step], 16 * (at % 2) + 8 * ((y + yr) % 2) + 4 * core)

        for half in range(2):
            place(came[yr].at[half], 16 * half + 8 * ((y + yr) % 2) + 4 * (1 - core))

    def conv_tile(tile, carry):
        lanes = lane_tile(first_tile + tile)
        for part in range(2):
            acc = [jnp.broadcast_to(bias[0:1, lanes], (16, LANES))] * 4
            for i in range(7):
                for src in range(4):
                    rows = feats[tile, src, pl.ds(5 + 16 * part + i, 16), :]
                    for col in range(4):
                        j = src - col + 3
                        acc[col] = acc[col] + kern[i, j : j + 1, lanes] * rows
            for col in range(4):
                at = pl.ds(64 * part + col, 16, stride=4)
                conv[tile, at, :] = acc[col]
        total[...] = total[...] + conv[tile]
        return carry

    lax.fori_loop(0, tiles, conv_tile, 0)


def conv_kernel(idx, *refs):
    kern, bias, feats, conv, total, turn = refs[10:]
    total[...] = jnp.zeros_like(total)
    place_and_convolve(
        idx, refs[:8], refs[8:10], kern, bias, feats, conv, turn, total, 0
    )


def conv_norm_kernel(idx, *refs):
    kern, bias, gain, shift, feats_low, conv_low, total_low = refs[10:17]
    normed, f_slice, u_slice, inv_slice = refs[17:21]
    feats, conv, turn, total, mean_ref, inv_ref = refs[21:]
    tiles = feats.shape[0]
    channels = 2 * tiles * LANES
    total[...] = total_low[...]
    place_and_convolve(
        idx, refs[:8], refs[8:10], kern, bias, feats, conv, turn, total, tiles
    )
    mean = jnp.sum(total[...], axis=-1, keepdims=True) / channels
    mean_ref[...] = jnp.broadcast_to(mean, mean_ref.shape)
    total[...] = jnp.zeros_like(total)
    halves = ((0, conv_low, feats_low), (tiles, conv, feats))

    def square_tile(tile, carry):
        low, high = conv_low[tile] - mean_ref[...], conv[tile] - mean_ref[...]
        total[...] = total[...] + (low * low + high * high)
        return carry

    lax.fori_loop(0, tiles, square_tile, 0)
    spread = jnp.sum(total[...], axis=-1, keepdims=True) / channels
    inv_ref[...] = jnp.broadcast_to(lax.rsqrt(spread + 1e-06), inv_ref.shape)

    def norm_tile(tile, carry):
        for start, values, _ in halves:
            lanes = lane_tile(start + tile)
            unit = (values[tile] - mean_ref[...]) * inv_ref[...]
            normed[:, lanes] = (unit * gain[0:1, lanes] + shift[0:1, lanes]).astype(BF16)
        return carry

    lax.fori_loop(0, tiles, norm_tile, 0)
    chip = idx[0] * 2 + idx[1]
    inv_slice[...] = inv_ref[...]
    for start, values, padded in halves:

        @pl.when((chip >= 4) == (start > 0))
        def _():
            for k in range(3):
                tile = (chip % 4) * 3 + k
                u_slice[k] = (values[tile] - mean_ref[...]) * inv_ref[...]
                f_slice[k] = padded[tile]


def cot_kernel(idx, *refs):
    layer_scale, cot_all, cot_slice = refs[8:]
    z, y, core = idx[0], idx[1], idx[2]
    chip = z * 2 + y
    own = lane_tile(chip * 3), lane_tile(chip * 3 + 1), lane_tile(chip * 3 + 2)
    for yr in range(2):
        for cr in range(2):
            for step in range(4):
                piece = refs[4 * cr + step].at[yr]
                at = (z + step + 3) % 4
                away = (at // 2 + core) % 2
                block = 4 * (at % 2) + 2 * ((y + yr) % 2) + (core + cr) % 2
                scaled = piece[...].astype(F32) * layer_scale[...]
                cot_all[sixteen(8 * away + block), :] = scaled.astype(BF16)

                @pl.when(away == 0)
                def _():
                    for k in range(3):
                        cot_slice[k, sixteen(block), :] = piece[:, own[k]].astype(F32)


def fold_kernel(gain, shift, weight, kern, shard, gain_dot, shift_dot, kern_out, shard_out):
    kern_out[...] = kern[...]
    shard_out[...] = shard[...]
    place = lax.broadcasted_iota(jnp.int32, (16, gain.shape[1]), 0)
    scale, offset = gain[...], shift[...]
    scale_hi = scale.astype(BF16).astype(F32)
    offset_hi = offset.astype(BF16).astype(F32)
    both = jnp.where(place == 0, scale_hi, 0.0)
    both = jnp.where(place == 1, scale - scale_hi, both)
    both = jnp.where(place == 2, offset_hi, both)
    both = jnp.where(place == 3, offset - offset_hi, both)
    product = jnp.dot(both.astype(BF16), weight[...], preferred_element_type=F32)
    gain_dot[...] = jnp.broadcast_to(product[0:1] + product[1:2], gain_dot.shape)
    shift_dot[...] = jnp.broadcast_to(product[2:3] + product[3:4], shift_dot.shape)


def hid_kernel(cot_all, weight, hid_grad):
    hid_grad[...] = contract(cot_all[...], weight[...], 1, 1)


def act_kernel(
    half, normed, weight, up_bias, hid_grad, gain_dot, shift_dot,
    hidden, act_grad, bias_grad, sums,
):
    tile = 256
    first = jnp.zeros((128, LANES), F32)
    second = jnp.zeros((128, LANES), F32)
    for start in range(0, hidden.shape[1], tile):
        at = slice(start, start + tile)
        plain = jnp.dot(normed[...], weight[:, at], preferred_element_type=F32)
        pre_act = plain + up_bias[0:1, at]
        cdf = 0.5 * (1.0 + lax.erf(pre_act * 0.7071067811865476))
        hidden[:, at] = (pre_act * cdf).astype(BF16)
        slope = cdf + pre_act * jnp.exp(-0.5 * pre_act * pre_act) * 0.3989422804014327
        act = (hid_grad[128 * half : 128 * half + 128, at] * slope).astype(BF16)
        act_grad[:, at] = act
        act = act.astype(F32)
        bias_grad[0:1, at] = jnp.sum(act, axis=0, keepdims=True)
        by_gain = act * gain_dot[0:1, at]
        by_unit = act * (plain - shift_dot[0:1, at])
        for lane in range(0, tile, LANES):
            first = first + by_gain[:, lane : lane + LANES]
            second = second + by_unit[:, lane : lane + LANES]
    ones = jnp.ones((8, LANES), F32)
    for row, part in ((0, first), (8, second)):
        sums[row : row + 8, :] = lax.dot_general(
            ones, part, (((1,), (1,)), ((), ())), precision=EXACT, preferred_element_type=F32
        )


def norm_grad_kernel(steps, idx, act_own, act_other, weight, sums_own, sums_other, keep, away):
    both = jnp.concatenate([act_other[...], act_own[...]], axis=0)
    for at, step in enumerate(steps):
        for yr in range(2):
            chip = 2 * ((idx[0] + step) % 4) + (idx[1] + yr) % 2
            rows = weight[pl.ds(pl.multiple_of(chip * 384, 128), 384), :]
            product = contract(both, rows, 1, 1)
            for ref, part, sums in ((away, 0, sums_other), (keep, 128, sums_own)):
                ref[at, yr, 0:128, :] = product[part : part + 128].astype(ref.dtype)
                ref[at, yr, 128:144, 0:128] = sums[...].astype(ref.dtype)
                ref[at, yr, 128:144, 128:384] = jnp.zeros((16, 256), ref.dtype)


def grad_kernel(left_own, left_other, right_own, right_other, *rest):
    left = jnp.concatenate([left_own[...], left_other[...]], axis=0).T
    right = jnp.concatenate([right_own[...], right_other[...]], axis=0)
    rest[-1][...] = contract(left, right, 1, 0)


def conv_back_kernel(
    idx, own, near_1, near_2, near_3, f_slice, u_slice, inv_slice, gain, kern, cot_slice,
    ig_keep, core_msg, small_keep, cg, turn, back, small,
):
    chip, y, core = idx[0] * 2 + idx[1], idx[1], idx[2]
    channels = gain.shape[1]

    def summed(rows, lanes):
        return (
            own[rows, lanes]
            + near_1[rows, lanes].astype(F32)
            + near_2[rows, lanes].astype(F32)
            + near_3[rows, lanes].astype(F32)
        )

    sums = summed(slice(128, 144), slice(0, 128))
    place = lax.broadcasted_iota(jnp.int32, (16, LANES), 0)

    def per_token(row):
        pick = jnp.where(place == row, 1.0 / channels, 0.0).astype(F32)
        return lax.dot_general(
            sums, pick, (((0,), (0,)), ((), ())), precision=EXACT, preferred_element_type=F32
        )

    mean_1, mean_2 = per_token(0), per_token(8)
    cg[:, :, 0:8, :] = jnp.zeros((3, 4, 8, LANES), F32)
    cg[:, :, 40:48, :] = jnp.zeros((3, 4, 8, LANES), F32)
    small[...] = jnp.zeros_like(small)
    for k in range(3):
        lanes = slice(k * LANES, (k + 1) * LANES)
        wide = lane_tile(chip * 3 + k)
        norm_grad = summed(slice(0, 128), lanes)
        unit = u_slice[k]
        scaled = norm_grad * gain[0:1, wide]
        grad = inv_slice[...] * (scaled - mean_1 - unit * mean_2)
        turn[k] = grad
        for col in range(4):
            cg[k, col, 8:40, :] = turn[k, pl.ds(col, 32, stride=4), :]
        small[56:57, lanes] = jnp.sum(norm_grad * unit, axis=0, keepdims=True)
        small[57:58, lanes] = jnp.sum(norm_grad, axis=0, keepdims=True)
        small[58:59, lanes] = jnp.sum(grad, axis=0, keepdims=True)
        for i in range(7):
            acc = [None] * 7
            for src in range(4):
                rows = f_slice[k, src, 5 + i : 37 + i, :]
                for col in range(4):
                    j = src - col + 3
                    term = cg[k, col, 8:40, :] * rows
                    acc[j] = term if acc[j] is None else acc[j] + term
            for j in range(7):
                small[8 * i + j : 8 * i + j + 1, lanes] = jnp.sum(acc[j], axis=0, keepdims=True)
        for part in range(2):
            acc = [cot_slice[k, pl.ds(64 * part + col, 16, stride=4), :] for col in range(4)]
            for i in range(7):
                for src in range(4):
                    start = 11 + 16 * part - i
                    rows = cg[k, src, start : start + 16, :]
                    for col in range(4):
                        j = col - src + 3
                        acc[col] = acc[col] + kern[i, j : j + 1, wide] * rows
            for col in range(4):
                back[k, pl.ds(64 * part + col, 16, stride=4), :] = acc[col]
        for half in range(2):
            for yr in range(2):
                for cr in range(2):
                    block = 4 * half + 2 * ((y + yr) % 2) + (core + cr) % 2
                    ref = core_msg if cr else ig_keep
                    ref[2 * half + yr, :, lanes] = back[k, sixteen(block), :].astype(BF16)
    for part in range(2):
        core_msg[4 + part] = small[sixteen(2 * (1 - core) + part), :].astype(BF16)
        small_keep[part] = small[sixteen(2 * core + part), :]


def route_kernel(idx, ig_keep, core_msg, small_keep, *msgs):
    z, core = idx[0], idx[2]
    total = [
        (small_keep[part] + core_msg[4 + part].astype(F32)).astype(BF16) for part in range(2)
    ]
    for step in range(4):
        at = (z + step + 3) % 4
        image, half = at // 2, at % 2
        for yr in range(2):
            kept, came = ig_keep[2 * half + yr], core_msg[2 * half + yr]
            msgs[step][yr] = jnp.where(image == core, kept, came)
        for part in range(2):
            msgs[step][2 + part] = total[part]


def place_kernel(idx, *refs):
    msgs, came, core_a, core_b = refs[:4], refs[4], refs[5], refs[6]
    tokens, kernel_grad, gain_grad, shift_grad, bias_grad = refs[7:]
    z, y, core = idx[0], idx[1], idx[2]
    for step in range(4):
        plane = (z + 4 - step) % 4
        for yr in range(2):
            chip = plane * 2 + (y + yr) % 2
            lanes = pl.ds(pl.multiple_of(chip * 384, 128), 384)
            block = (came[step, 0] if yr else msgs[step][0]).astype(F32)
            for row in range(4):
                tokens[row, :, lanes] = block[4 * row : 4 * row + 4].astype(BF16)
            for part in range(2):
                mine = (came[step, 1 + part] if yr else msgs[step][2 + part]).astype(F32)
                other = (core_b[step, part] if yr else core_a[step, part]).astype(F32)
                low = jnp.where(core == 0, mine, other)
                high = jnp.where(core == 0, other, mine)
                for sub in range(2):
                    at = 2 * part + sub
                    rows = slice(8 * sub, 8 * sub + 7)
                    kernel_grad[at, :, lanes] = low[rows]
                    if at < 3:
                        kernel_grad[4 + at, :, lanes] = high[rows]
                    else:
                        gain_grad[0:1, lanes] = high[8:9]
                        shift_grad[0:1, lanes] = high[9:10]
                        bias_grad[0:1, lanes] = high[10:11]


def shape(dims, dtype):
    return jax.ShapeDtypeStruct(dims, dtype)


def call(kernel, micros, room, out_shape, inputs, scratch=(), scalars=1):
    return pl.pallas_call(
        kernel,
        out_shape=out_shape,
        in_specs=[SSPEC] * scalars + [VSPEC] * (len(inputs) - scalars),
        out_specs=jax.tree.map(lambda _: VSPEC, out_shape),
        scratch_shapes=list(scratch),
        compiler_params=pltpu.CompilerParams(vmem_limit_bytes=room * MIB),
        cost_estimate=cost(micros),
    )(*inputs)


def cost(micros):
    return pl.CostEstimate(
        flops=int(micros * 1.1e9), bytes_accessed=int(micros * 3.4e6), transcendentals=0
    )


def half_gradient(part, left, right, tile, so_far=None):
    rows, cols = left[0].shape[1], right[0].shape[1]
    steps = rows // 2 // tile
    left_spec = pl.BlockSpec((128, tile), lambda m: (0, part * steps + m))
    right_spec = pl.BlockSpec((128, cols), lambda m: (0, 0))
    whole = right[1] is right[0]
    other_spec = pl.BlockSpec((128, cols), lambda m: (1, 0)) if whole else right_spec
    extra = () if so_far is None else (so_far,)
    return pl.pallas_call(
        grad_kernel,
        grid=(steps,),
        out_shape=shape((rows, cols), F32),
        in_specs=[left_spec, left_spec, right_spec, other_spec]
        + [pl.BlockSpec(memory_space=pl.ANY)] * len(extra),
        out_specs=pl.BlockSpec((tile, cols), lambda m: (part * steps + m, 0)),
        input_output_aliases={4: 0} if extra else {},
        compiler_params=pltpu.CompilerParams(vmem_limit_bytes=16 * MIB),
        cost_estimate=cost(2.5),
    )(*left, *right, *extra)


def sliced_device(
    features,
    cotangent,
    depth_kernel,
    depth_bias,
    norm_gain,
    norm_shift,
    up_weight,
    up_bias,
    down_weight,
    layer_scale,
):
    channels, hidden_dev = up_weight.shape
    tiles = channels // LANES
    index = lax.axis_index("rows")
    z, y, core = index // 4, (index // 2) % 2, index % 2
    idx = jnp.stack([z, y, core]).astype(jnp.int32)
    bias_row, gain_row = depth_bias.reshape(1, channels), norm_gain.reshape(1, channels)
    shift_row, scale_row = norm_shift.reshape(1, channels), layer_scale.reshape(1, channels)
    up_bias_row = up_bias.reshape(1, hidden_dev)

    cot_shard = cotangent.reshape(16, channels)
    planes, across = gather_chips(features)
    gain_dot, shift_dot, kern, own_shard = call(
        fold_kernel,
        1.5,
        10,
        (
            shape((8, hidden_dev), F32),
            shape((8, hidden_dev), F32),
            shape(depth_kernel.shape, F32),
            shape(features.shape, BF16),
        ),
        (gain_row, shift_row, up_weight, depth_kernel, features),
        scalars=0,
    )
    planes = [own_shard] + planes[1:]
    picks = [(2 * (1 - core) + half + 1 - z) % 4 for half in range(2)]
    chosen = [
        jnp.stack([lax.select_n(pick, *pieces) for pick in picks]) for pieces in (planes, across)
    ]
    with jax.named_scope("feat_core"):
        feat_came = [send(pieces, C_PAIRS) for pieces in chosen]
    with jax.named_scope("cot_y"):
        cot_pair = jnp.stack([cot_shard, send(cot_shard, Y_PAIRS)])
    with jax.named_scope("cot_z"):
        cot_late = after(cot_pair, tuple(planes[1:]))
        cot_planes = [cot_pair] + [send(cot_late, z_pairs(step)) for step in (1, 2, 3)]
    half_tiles = tiles // 2
    turn = VMEM((4, 16, LANES), F32)
    square = VMEM((128, LANES), F32)
    conv_args = (*planes, *across, *feat_came, kern, bias_row)
    feats_low, conv_low, total_low = call(
        conv_kernel,
        8.0,
        12,
        (
            shape((half_tiles, 4, 48, LANES), F32),
            shape((half_tiles, 128, LANES), F32),
            shape((128, LANES), F32),
        ),
        (after(idx, (cot_planes[1], cot_planes[3])), *conv_args),
        (turn,),
    )
    normed, f_slice, u_slice, inv_slice = call(
        conv_norm_kernel,
        8.0,
        12,
        (
            shape((128, channels), BF16),
            shape((3, 4, 48, LANES), F32),
            shape((3, 128, LANES), F32),
            shape((128, LANES), F32),
        ),
        (
            idx, *conv_args, gain_row, shift_row,
            feats_low, conv_low, total_low,
        ),
        (
            VMEM((half_tiles, 4, 48, LANES), F32),
            VMEM((half_tiles, 128, LANES), F32),
            turn,
            square,
            square,
            square,
        ),
    )
    with jax.named_scope("cot_core"):
        cot_came = [send(after(plane, inv_slice), C_PAIRS) for plane in cot_planes]
    normed_other = send(normed, C_PAIRS)
    cot_all, cot_slice = call(
        cot_kernel,
        1.5,
        8,
        (shape((256, channels), BF16), shape((3, 128, LANES), F32)),
        (idx, *cot_planes, *cot_came, scale_row),
    )
    hid_grad = call(
        hid_kernel, 1.5, 8, shape((256, hidden_dev), F32), (cot_all, down_weight), scalars=0
    )
    halves = [
        call(
            functools.partial(act_kernel, half),
            1.7,
            12,
            (
                shape((128, hidden_dev), BF16),
                shape((128, hidden_dev), BF16),
                shape((1, hidden_dev), F32),
                shape((16, LANES), F32),
            ),
            (value, up_weight, up_bias_row, hid_grad, gain_dot, shift_dot),
            scalars=0,
        )
        for half, value in enumerate((normed, normed_other))
    ]
    hidden = [part[0] for part in halves]
    act_grad = [part[1] for part in halves]
    sums = [part[3] for part in halves]

    arrived, came_at, keep_at, across_at = {}, {}, {}, {}
    for pair in ((1, 2), (3, 0)):
        keep, away = call(
            functools.partial(norm_grad_kernel, pair),
            1.6,
            10,
            (shape((2, 2, 144, 384), F32), shape((2, 2, 144, 384), BF16)),
            (idx, *act_grad, up_weight, *sums),
        )
        came = send(away, C_PAIRS)
        for at, step in enumerate(pair):
            came_at[step], keep_at[step] = came[at].astype(F32), keep[at]
            across_at[step] = send((keep[at, 1] + came_at[step][1]).astype(BF16), Y_PAIRS)
    cots = (cot_all, cot_all)
    down_low = half_gradient(0, after(tuple(hidden), came), cots, 128)
    for step in (1, 2, 3, 0):
        total = keep_at[step][0] + came_at[step][0]
        if step == 2:
            total = after(total, down_low[0, 0])
        total = total + across_at[step].astype(F32)
        if step:
            total = send(total.astype(BF16), flipped(z_pairs(step)))
        arrived[step] = total
    down_grad = half_gradient(1, after(tuple(hidden), across_at[0]), cots, 128, down_low)
    ig_keep, core_msg, small_keep = call(
        conv_back_kernel,
        2.2,
        12,
        (shape((4, 16, 384), BF16), shape((6, 16, 384), BF16), shape((2, 16, 384), F32)),
        (
            after(idx, down_grad[0, 0]), arrived[0], arrived[1], arrived[2], arrived[3], f_slice, u_slice, inv_slice,
            gain_row, kern, cot_slice,
        ),
        (
            VMEM((3, 4, 48, LANES), F32),
            VMEM((3, 128, LANES), F32),
            VMEM((3, 128, LANES), F32),
            VMEM((64, 384), F32),
        ),
    )
    core_msg = send(core_msg, C_PAIRS)
    msgs = call(
        route_kernel,
        0.5,
        4,
        tuple(shape((4, 16, 384), BF16) for _ in range(4)),
        (idx, ig_keep, core_msg, small_keep),
    )
    msgs = [msgs[0]] + [send(msgs[step], flipped(z_pairs(step))) for step in (1, 2, 3)]
    up_low = half_gradient(0, after((normed, normed_other), msgs[1]), act_grad, 512)
    came = send(jnp.stack([msg[1:4] for msg in msgs]), Y_PAIRS)
    core_a = send(jnp.stack([msg[2:4] for msg in msgs]), C_PAIRS)
    up_grad = half_gradient(1, after((normed, normed_other), core_a), act_grad, 512, up_low)
    core_b = send(came[:, 1:3], C_PAIRS)
    row = shape((1, channels), F32)
    tokens, kernel_grad, gain_grad, shift_grad, depth_bias_grad = call(
        place_kernel,
        0.8,
        8,
        (shape((4, 4, channels), BF16), shape((7, 7, channels), F32), row, row, row),
        (idx, *msgs, came, core_a, core_b),
    )
    return (
        tokens,
        up_grad,
        (halves[0][2] + halves[1][2]).reshape(hidden_dev),
        down_grad,
        kernel_grad,
        depth_bias_grad.reshape(channels),
        gain_grad.reshape(channels),
        shift_grad.reshape(channels),
    )


def on_device(features, *rest):
    rows_dev, cols, channels = features.shape
    fits = lax.axis_size("rows") == 16 and rows_dev == 4 and cols == 4 and channels == 3072
    return (sliced_device if fits else generic_device)(features, *rest)


def solution(mesh):
    in_specs = (
        P(("groups", "rows"), None, None),
        P(("groups", "rows"), None, None),
        P(),
        P(),
        P(),
        P(),
        P(None, "rows"),
        P("rows"),
        P("rows", None),
        P(),
    )
    out_specs = (
        P(("groups", "rows"), None, None),
        P("groups", "rows"),
        P(("groups", "rows")),
        P(("groups", "rows"), None),
        P("groups", None, None),
        P("groups"),
        P("groups"),
        P("groups"),
    )
    return jax.shard_map(
        on_device, mesh=mesh, in_specs=in_specs, out_specs=out_specs, check_vma=False
    )
```

```python
import functools

import jax
import jax.numpy as jnp
from jax import lax
from jax.experimental import pallas as pl
from jax.experimental.pallas import tpu as pltpu
from jax.sharding import PartitionSpec as P

IMG_ROWS = 32
BF16 = jnp.bfloat16
F32 = jnp.float32


def stages_of(count):
    sizes = []
    chips = count // 2
    while chips % 4 == 0 and chips > 4:
        sizes.append(4)
        chips //= 4
    if chips > 1:
        sizes.append(chips)
    out = [(1, 2)]
    stride = 2
    for size in reversed(sizes):
        out.insert(0, (stride, size))
        stride *= size
    return out


def from_ahead(count, stride, size, step):
    pairs = []
    for i in range(count):
        digit = (i // stride) % size
        src = i + ((digit + step) % size - digit) * stride
        pairs.append((src, i))
    return pairs


def send(value, pairs):
    return lax.ppermute(value, "rows", pairs)


def gather_stage(value, count, stride, size):
    parts = [value]
    for step in range(1, size):
        parts.append(send(value, from_ahead(count, stride, size, step)))
    return jnp.stack(parts)


def scatter_stage(value, count, stride, size):
    total = value[0].astype(F32)
    for step in range(1, size):
        back = [(dst, src) for src, dst in from_ahead(count, stride, size, step)]
        total = total + send(value[step], back).astype(F32)
    return total


def gelu_parts(pre_act):
    cdf = 0.5 * (1.0 + jax.scipy.special.erf(pre_act * 0.7071067811865476))
    slope = cdf + pre_act * jnp.exp(-0.5 * pre_act * pre_act) * 0.3989422804014327
    return pre_act * cdf, slope


def contract(left, right, left_dim, right_dim):
    return lax.dot_general(
        left, right, (((left_dim,), (right_dim,)), ((), ())), preferred_element_type=F32
    )


def extended(cells, width, fwd, bwd):
    head = lax.slice_in_dim(cells, 0, width, axis=0)
    tail = lax.slice_in_dim(cells, cells.shape[0] - width, cells.shape[0], axis=0)
    return jnp.concatenate([send(tail, fwd), cells, send(head, bwd)], axis=0)


def generic_device(
    features,
    cotangent,
    depth_kernel,
    depth_bias,
    norm_gain,
    norm_shift,
    up_weight,
    up_bias,
    down_weight,
    layer_scale,
):
    rows_dev, cols, channels = features.shape
    count = lax.axis_size("rows")
    stages = stages_of(count)
    shard = rows_dev * cols
    half_image = IMG_ROWS // 2
    crossing = [
        (i, (i + 1) % count)
        for i in range(count)
        if ((i + 1) * rows_dev - half_image) % IMG_ROWS != 0
    ]
    fwd = crossing
    bwd = [(b, a) for a, b in crossing]
    pieces = 2
    width = channels // pieces

    def gather(value):
        outs = []
        for p in range(pieces):
            part = value[:, p * width : (p + 1) * width]
            for stride, size in stages:
                part = gather_stage(part, count, stride, size)
            outs.append(part.reshape(shard * count, width))
        return outs

    near = extended(features, 3, fwd, bwd).astype(F32)
    cot_scaled = (
        (cotangent.astype(F32) * layer_scale).astype(BF16).reshape(shard, channels)
    )
    cot_all = gather(cot_scaled)
    padded = jnp.pad(near, ((0, 0), (3, 3), (0, 0)))
    conv_out = jnp.zeros((rows_dev, cols, channels), F32)
    for i in range(7):
        for j in range(7):
            conv_out = conv_out + depth_kernel[i, j] * padded[i : i + rows_dev, j : j + cols]
    conv_out = conv_out + depth_bias
    row_mean = jnp.mean(conv_out, axis=-1, keepdims=True)
    centred = conv_out - row_mean
    inv_std = lax.rsqrt(jnp.mean(centred * centred, axis=-1, keepdims=True) + 1e-06)
    unit_norm = centred * inv_std
    normed = (unit_norm * norm_gain + norm_shift).astype(BF16).reshape(shard, channels)
    normed_all = gather(normed)

    hid_grad = sum(
        contract(cot_all[p], down_weight[:, p * width : (p + 1) * width], 1, 1)
        for p in range(pieces)
    )
    pre_act = up_bias + sum(
        contract(normed_all[p], up_weight[p * width : (p + 1) * width], 1, 0)
        for p in range(pieces)
    )
    value, slope = gelu_parts(pre_act)
    hidden = value.astype(BF16)
    act_grad = (hid_grad * slope).astype(BF16)

    norm_parts = []
    for p in range(pieces):
        part = contract(act_grad, up_weight[p * width : (p + 1) * width], 1, 1).astype(BF16)
        lead = [size for _, size in reversed(stages)]
        part = part.reshape(*lead, shard, width)
        for stride, size in reversed(stages):
            part = scatter_stage(part, count, stride, size)
            if stride != stages[0][0]:
                part = part.astype(BF16)
        norm_parts.append(part)
    norm_grad = jnp.concatenate(norm_parts, axis=-1).reshape(rows_dev, cols, channels)

    up_bias_grad = jnp.sum(act_grad.astype(F32), axis=0)
    down_grad = jnp.concatenate([contract(hidden, c, 0, 0) for c in cot_all], axis=1)
    up_grad = jnp.concatenate([contract(n, act_grad, 0, 0) for n in normed_all], axis=0)

    gain_part = jnp.sum(norm_grad * unit_norm, axis=(0, 1))
    shift_part = jnp.sum(norm_grad, axis=(0, 1))
    scaled = norm_grad * norm_gain
    conv_grad = inv_std * (
        scaled
        - jnp.mean(scaled, axis=-1, keepdims=True)
        - unit_norm * jnp.mean(scaled * unit_norm, axis=-1, keepdims=True)
    )
    bias_part = jnp.sum(conv_grad, axis=(0, 1))
    rows_out = [
        jnp.sum(conv_grad * padded[i : i + rows_dev, j : j + cols], axis=(0, 1))
        for i in range(7)
        for j in range(7)
    ]
    near_grad = extended(conv_grad.astype(BF16), 3, fwd, bwd).astype(F32)
    grad_padded = jnp.pad(near_grad, ((0, 0), (3, 3), (0, 0)))

    chips = count // 2
    per = -(-52 // chips)
    small = jnp.stack(rows_out + [gain_part, shift_part, bias_part])
    small = jnp.pad(small, ((0, per * chips - 52), (0, 0)))
    half = channels // 2
    small = small.reshape(chips, per, 2, half).transpose(2, 0, 1, 3)
    core = lax.axis_index("rows") % 2
    swapped = jnp.where(core == 0, small, small[::-1])
    swapped = swapped.astype(BF16)
    mine = swapped[0].astype(F32) + send(
        swapped[1], from_ahead(count, 1, 2, 1)
    ).astype(F32)
    mine = mine.astype(BF16)
    chip = lax.axis_index("rows") // 2
    ahead = jnp.roll(mine, -chip, axis=0)
    total = ahead[0].astype(F32)
    for step in range(1, chips):
        back = [(dst, src) for src, dst in from_ahead(count, 2, chips, step)]
        total = total + send(ahead[step], back).astype(F32)
    total = total.astype(BF16)
    every = [total] + [
        send(total, from_ahead(count, 2, chips, step)) for step in range(1, chips)
    ]
    every = jnp.roll(jnp.stack(every), chip, axis=0)
    other = send(every, from_ahead(count, 1, 2, 1))
    both = jnp.where(
        core == 0,
        jnp.concatenate([every, other], axis=-1),
        jnp.concatenate([other, every], axis=-1),
    )
    both = both.reshape(per * chips, channels).astype(F32)
    kernel_grad = both[:49].reshape(7, 7, channels)
    gain_grad, shift_grad, depth_bias_grad = both[49], both[50], both[51]

    back_term = jnp.zeros((rows_dev, cols, channels), F32)
    for i in range(7):
        for j in range(7):
            back_term = back_term + depth_kernel[i, j] * grad_padded[
                6 - i : 6 - i + rows_dev, 6 - j : 6 - j + cols
            ]
    input_grad = (cotangent.astype(F32) + back_term).astype(BF16)
    return (
        input_grad,
        up_grad,
        up_bias_grad,
        down_grad,
        kernel_grad,
        depth_bias_grad,
        gain_grad,
        shift_grad,
    )


LANES = 128
VMEM = pltpu.VMEM
VSPEC = pl.BlockSpec(memory_space=pltpu.VMEM)
SSPEC = pl.BlockSpec(memory_space=pltpu.SMEM)
EXACT = lax.Precision.HIGHEST
MIB = 1024 * 1024


def z_pairs(step):
    return from_ahead(16, 4, 4, step)


def flipped(pairs):
    return [(dst, src) for src, dst in pairs]


Y_PAIRS = from_ahead(16, 2, 2, 1)
C_PAIRS = from_ahead(16, 1, 2, 1)


def after(value, other):
    return lax.optimization_barrier((value, other))[0]


def gather_chips(shard):
    with jax.named_scope("feat_z"):
        planes = [shard] + [send(shard, z_pairs(step)) for step in (1, 2, 3)]
    with jax.named_scope("feat_y"):
        return planes, [send(plane, Y_PAIRS) for plane in planes]


def lane_tile(tile):
    return pl.ds(pl.multiple_of(tile * LANES, LANES), LANES)


def sixteen(block):
    return pl.ds(pl.multiple_of(block * 16, 16), 16)


def place_and_convolve(idx, pieces, came, kern, bias, feats, conv, turn, total, first_tile):
    z, y, core = idx[0], idx[1], idx[2]
    tiles = feats.shape[0]
    edge = jnp.zeros((tiles, 4, 8, LANES), F32)
    feats[:, :, 0:8, :] = edge
    feats[:, :, 40:48, :] = edge

    def place(piece, row):
        for tile in range(tiles):
            lanes = slice((first_tile + tile) * LANES, (first_tile + tile + 1) * LANES)
            for r in range(4):
                turn[tile % 4, 4 * r : 4 * r + 4, :] = piece[r, :, lanes].astype(F32)
            for col in range(4):
                feats[tile, col, pl.ds(8 + row, 4), :] = turn[
                    tile % 4, pl.ds(col, 4, stride=4), :
                ]

    for yr in range(2):
        for step in range(4):
            at = (z + step + 3) % 4

            @pl.when(at // 2 == core)
            def _():
                place(pieces[4 * yr + step], 16 * (at % 2) + 8 * ((y + yr) % 2) + 4 * core)

        for half in range(2):
            place(came[yr].at[half], 16 * half + 8 * ((y + yr) % 2) + 4 * (1 - core))

    def conv_tile(tile, carry):
        lanes = lane_tile(first_tile + tile)
        for part in range(2):
            acc = [jnp.broadcast_to(bias[0:1, lanes], (16, LANES))] * 4
            for i in range(7):
                for src in range(4):
                    rows = feats[tile, src, pl.ds(5 + 16 * part + i, 16), :]
                    for col in range(4):
                        j = src - col + 3
                        acc[col] = acc[col] + kern[i, j : j + 1, lanes] * rows
            for col in range(4):
                at = pl.ds(64 * part + col, 16, stride=4)
                conv[tile, at, :] = acc[col]
        total[...] = total[...] + conv[tile]
        return carry

    lax.fori_loop(0, tiles, conv_tile, 0)


def conv_kernel(idx, *refs):
    kern, bias, feats, conv, total, turn = refs[10:]
    total[...] = jnp.zeros_like(total)
    place_and_convolve(
        idx, refs[:8], refs[8:10], kern, bias, feats, conv, turn, total, 0
    )


def conv_norm_kernel(idx, *refs):
    kern, bias, gain, shift, feats_low, conv_low, total_low = refs[10:17]
    normed, f_slice, u_slice, inv_slice = refs[17:21]
    feats, conv, turn, total, mean_ref, inv_ref = refs[21:]
    tiles = feats.shape[0]
    channels = 2 * tiles * LANES
    total[...] = total_low[...]
    place_and_convolve(
        idx, refs[:8], refs[8:10], kern, bias, feats, conv, turn, total, tiles
    )
    mean = jnp.sum(total[...], axis=-1, keepdims=True) / channels
    mean_ref[...] = jnp.broadcast_to(mean, mean_ref.shape)
    total[...] = jnp.zeros_like(total)
    halves = ((0, conv_low, feats_low), (tiles, conv, feats))

    def square_tile(tile, carry):
        low, high = conv_low[tile] - mean_ref[...], conv[tile] - mean_ref[...]
        total[...] = total[...] + (low * low + high * high)
        return carry

    lax.fori_loop(0, tiles, square_tile, 0)
    spread = jnp.sum(total[...], axis=-1, keepdims=True) / channels
    inv_ref[...] = jnp.broadcast_to(lax.rsqrt(spread + 1e-06), inv_ref.shape)

    def norm_tile(tile, carry):
        for start, values, _ in halves:
            lanes = lane_tile(start + tile)
            unit = (values[tile] - mean_ref[...]) * inv_ref[...]
            normed[:, lanes] = (unit * gain[0:1, lanes] + shift[0:1, lanes]).astype(BF16)
        return carry

    lax.fori_loop(0, tiles, norm_tile, 0)
    chip = idx[0] * 2 + idx[1]
    inv_slice[...] = inv_ref[...]
    for start, values, padded in halves:

        @pl.when((chip >= 4) == (start > 0))
        def _():
            for k in range(3):
                tile = (chip % 4) * 3 + k
                u_slice[k] = (values[tile] - mean_ref[...]) * inv_ref[...]
                f_slice[k] = padded[tile]


def cot_kernel(idx, *refs):
    layer_scale, cot_all, cot_slice = refs[8:]
    z, y, core = idx[0], idx[1], idx[2]
    chip = z * 2 + y
    own = lane_tile(chip * 3), lane_tile(chip * 3 + 1), lane_tile(chip * 3 + 2)
    for yr in range(2):
        for cr in range(2):
            for step in range(4):
                piece = refs[4 * cr + step].at[yr]
                at = (z + step + 3) % 4
                away = (at // 2 + core) % 2
                block = 4 * (at % 2) + 2 * ((y + yr) % 2) + (core + cr) % 2
                scaled = piece[...].astype(F32) * layer_scale[...]
                cot_all[sixteen(8 * away + block), :] = scaled.astype(BF16)

                @pl.when(away == 0)
                def _():
                    for k in range(3):
                        cot_slice[k, sixteen(block), :] = piece[:, own[k]].astype(F32)


def fold_kernel(gain, shift, weight, kern, shard, gain_dot, shift_dot, kern_out, shard_out):
    kern_out[...] = kern[...]
    shard_out[...] = shard[...]
    place = lax.broadcasted_iota(jnp.int32, (16, gain.shape[1]), 0)
    scale, offset = gain[...], shift[...]
    scale_hi = scale.astype(BF16).astype(F32)
    offset_hi = offset.astype(BF16).astype(F32)
    both = jnp.where(place == 0, scale_hi, 0.0)
    both = jnp.where(place == 1, scale - scale_hi, both)
    both = jnp.where(place == 2, offset_hi, both)
    both = jnp.where(place == 3, offset - offset_hi, both)
    product = jnp.dot(both.astype(BF16), weight[...], preferred_element_type=F32)
    gain_dot[...] = jnp.broadcast_to(product[0:1] + product[1:2], gain_dot.shape)
    shift_dot[...] = jnp.broadcast_to(product[2:3] + product[3:4], shift_dot.shape)


def hid_kernel(cot_all, weight, hid_grad):
    hid_grad[...] = contract(cot_all[...], weight[...], 1, 1)


def act_kernel(
    half, normed, weight, up_bias, hid_grad, gain_dot, shift_dot,
    hidden, act_grad, bias_grad, sums,
):
    tile = 256
    first = jnp.zeros((128, LANES), F32)
    second = jnp.zeros((128, LANES), F32)
    for start in range(0, hidden.shape[1], tile):
        at = slice(start, start + tile)
        plain = jnp.dot(normed[...], weight[:, at], preferred_element_type=F32)
        pre_act = plain + up_bias[0:1, at]
        cdf = 0.5 * (1.0 + lax.erf(pre_act * 0.7071067811865476))
        hidden[:, at] = (pre_act * cdf).astype(BF16)
        slope = cdf + pre_act * jnp.exp(-0.5 * pre_act * pre_act) * 0.3989422804014327
        act = (hid_grad[128 * half : 128 * half + 128, at] * slope).astype(BF16)
        act_grad[:, at] = act
        act = act.astype(F32)
        bias_grad[0:1, at] = jnp.sum(act, axis=0, keepdims=True)
        by_gain = act * gain_dot[0:1, at]
        by_unit = act * (plain - shift_dot[0:1, at])
        for lane in range(0, tile, LANES):
            first = first + by_gain[:, lane : lane + LANES]
            second = second + by_unit[:, lane : lane + LANES]
    ones = jnp.ones((8, LANES), F32)
    for row, part in ((0, first), (8, second)):
        sums[row : row + 8, :] = lax.dot_general(
            ones, part, (((1,), (1,)), ((), ())), precision=EXACT, preferred_element_type=F32
        )


def norm_grad_kernel(steps, idx, act_own, act_other, weight, sums_own, sums_other, keep, away):
    both = jnp.concatenate([act_other[...], act_own[...]], axis=0)
    for at, step in enumerate(steps):
        for yr in range(2):
            chip = 2 * ((idx[0] + step) % 4) + (idx[1] + yr) % 2
            rows = weight[pl.ds(pl.multiple_of(chip * 384, 128), 384), :]
            product = contract(both, rows, 1, 1)
            for ref, part, sums in ((away, 0, sums_other), (keep, 128, sums_own)):
                ref[at, yr, 0:128, :] = product[part : part + 128].astype(ref.dtype)
                ref[at, yr, 128:144, 0:128] = sums[...].astype(ref.dtype)
                ref[at, yr, 128:144, 128:384] = jnp.zeros((16, 256), ref.dtype)


def grad_kernel(left_own, left_other, right_own, right_other, *rest):
    left = jnp.concatenate([left_own[...], left_other[...]], axis=0).T
    right = jnp.concatenate([right_own[...], right_other[...]], axis=0)
    rest[-1][...] = contract(left, right, 1, 0)


def conv_back_kernel(
    idx, own, near_1, near_2, near_3, f_slice, u_slice, inv_slice, gain, kern, cot_slice,
    ig_keep, core_msg, small_keep, cg, turn, back, small,
):
    chip, y, core = idx[0] * 2 + idx[1], idx[1], idx[2]
    channels = gain.shape[1]

    def summed(rows, lanes):
        return (
            own[rows, lanes]
            + near_1[rows, lanes].astype(F32)
            + near_2[rows, lanes].astype(F32)
            + near_3[rows, lanes].astype(F32)
        )

    sums = summed(slice(128, 144), slice(0, 128))
    place = lax.broadcasted_iota(jnp.int32, (16, LANES), 0)

    def per_token(row):
        pick = jnp.where(place == row, 1.0 / channels, 0.0).astype(F32)
        return lax.dot_general(
            sums, pick, (((0,), (0,)), ((), ())), precision=EXACT, preferred_element_type=F32
        )

    mean_1, mean_2 = per_token(0), per_token(8)
    cg[:, :, 0:8, :] = jnp.zeros((3, 4, 8, LANES), F32)
    cg[:, :, 40:48, :] = jnp.zeros((3, 4, 8, LANES), F32)
    small[...] = jnp.zeros_like(small)
    for k in range(3):
        lanes = slice(k * LANES, (k + 1) * LANES)
        wide = lane_tile(chip * 3 + k)
        norm_grad = summed(slice(0, 128), lanes)
        unit = u_slice[k]
        scaled = norm_grad * gain[0:1, wide]
        grad = inv_slice[...] * (scaled - mean_1 - unit * mean_2)
        turn[k] = grad
        for col in range(4):
            cg[k, col, 8:40, :] = turn[k, pl.ds(col, 32, stride=4), :]
        small[56:57, lanes] = jnp.sum(norm_grad * unit, axis=0, keepdims=True)
        small[57:58, lanes] = jnp.sum(norm_grad, axis=0, keepdims=True)
        small[58:59, lanes] = jnp.sum(grad, axis=0, keepdims=True)
        for i in range(7):
            acc = [None] * 7
            for src in range(4):
                rows = f_slice[k, src, 5 + i : 37 + i, :]
                for col in range(4):
                    j = src - col + 3
                    term = cg[k, col, 8:40, :] * rows
                    acc[j] = term if acc[j] is None else acc[j] + term
            for j in range(7):
                small[8 * i + j : 8 * i + j + 1, lanes] = jnp.sum(acc[j], axis=0, keepdims=True)
        for part in range(2):
            acc = [cot_slice[k, pl.ds(64 * part + col, 16, stride=4), :] for col in range(4)]
            for i in range(7):
                for src in range(4):
                    start = 11 + 16 * part - i
                    rows = cg[k, src, start : start + 16, :]
                    for col in range(4):
                        j = col - src + 3
                        acc[col] = acc[col] + kern[i, j : j + 1, wide] * rows
            for col in range(4):
                back[k, pl.ds(64 * part + col, 16, stride=4), :] = acc[col]
        for half in range(2):
            for yr in range(2):
                for cr in range(2):
                    block = 4 * half + 2 * ((y + yr) % 2) + (core + cr) % 2
                    ref = core_msg if cr else ig_keep
                    ref[2 * half + yr, :, lanes] = back[k, sixteen(block), :].astype(BF16)
    for part in range(2):
        core_msg[4 + part] = small[sixteen(2 * (1 - core) + part), :].astype(BF16)
        small_keep[part] = small[sixteen(2 * core + part), :]


def route_kernel(idx, ig_keep, core_msg, small_keep, *msgs):
    z, core = idx[0], idx[2]
    total = [
        (small_keep[part] + core_msg[4 + part].astype(F32)).astype(BF16) for part in range(2)
    ]
    for step in range(4):
        at = (z + step + 3) % 4
        image, half = at // 2, at % 2
        for yr in range(2):
            kept, came = ig_keep[2 * half + yr], core_msg[2 * half + yr]
            msgs[step][yr] = jnp.where(image == core, kept, came)
        for part in range(2):
            msgs[step][2 + part] = total[part]


def place_kernel(idx, *refs):
    msgs, came, core_a, core_b = refs[:4], refs[4], refs[5], refs[6]
    tokens, kernel_grad, gain_grad, shift_grad, bias_grad = refs[7:]
    z, y, core = idx[0], idx[1], idx[2]
    for step in range(4):
        plane = (z + 4 - step) % 4
        for yr in range(2):
            chip = plane * 2 + (y + yr) % 2
            lanes = pl.ds(pl.multiple_of(chip * 384, 128), 384)
            block = (came[step, 0] if yr else msgs[step][0]).astype(F32)
            for row in range(4):
                tokens[row, :, lanes] = block[4 * row : 4 * row + 4].astype(BF16)
            for part in range(2):
                mine = (came[step, 1 + part] if yr else msgs[step][2 + part]).astype(F32)
                other = (core_b[step, part] if yr else core_a[step, part]).astype(F32)
                low = jnp.where(core == 0, mine, other)
                high = jnp.where(core == 0, other, mine)
                for sub in range(2):
                    at = 2 * part + sub
                    rows = slice(8 * sub, 8 * sub + 7)
                    kernel_grad[at, :, lanes] = low[rows]
                    if at < 3:
                        kernel_grad[4 + at, :, lanes] = high[rows]
                    else:
                        gain_grad[0:1, lanes] = high[8:9]
                        shift_grad[0:1, lanes] = high[9:10]
                        bias_grad[0:1, lanes] = high[10:11]


def shape(dims, dtype):
    return jax.ShapeDtypeStruct(dims, dtype)


def call(kernel, micros, room, out_shape, inputs, scratch=(), scalars=1):
    return pl.pallas_call(
        kernel,
        out_shape=out_shape,
        in_specs=[SSPEC] * scalars + [VSPEC] * (len(inputs) - scalars),
        out_specs=jax.tree.map(lambda _: VSPEC, out_shape),
        scratch_shapes=list(scratch),
        compiler_params=pltpu.CompilerParams(vmem_limit_bytes=room * MIB),
        cost_estimate=cost(micros),
    )(*inputs)


def cost(micros):
    return pl.CostEstimate(
        flops=int(micros * 1.1e9), bytes_accessed=int(micros * 3.4e6), transcendentals=0
    )


def half_gradient(part, left, right, tile, so_far=None):
    rows, cols = left[0].shape[1], right[0].shape[1]
    steps = rows // 2 // tile
    left_spec = pl.BlockSpec((128, tile), lambda m: (0, part * steps + m))
    right_spec = pl.BlockSpec((128, cols), lambda m: (0, 0))
    whole = right[1] is right[0]
    other_spec = pl.BlockSpec((128, cols), lambda m: (1, 0)) if whole else right_spec
    extra = () if so_far is None else (so_far,)
    return pl.pallas_call(
        grad_kernel,
        grid=(steps,),
        out_shape=shape((rows, cols), F32),
        in_specs=[left_spec, left_spec, right_spec, other_spec]
        + [pl.BlockSpec(memory_space=pl.ANY)] * len(extra),
        out_specs=pl.BlockSpec((tile, cols), lambda m: (part * steps + m, 0)),
        input_output_aliases={4: 0} if extra else {},
        compiler_params=pltpu.CompilerParams(vmem_limit_bytes=16 * MIB),
        cost_estimate=cost(2.5),
    )(*left, *right, *extra)


def sliced_device(
    features,
    cotangent,
    depth_kernel,
    depth_bias,
    norm_gain,
    norm_shift,
    up_weight,
    up_bias,
    down_weight,
    layer_scale,
):
    channels, hidden_dev = up_weight.shape
    tiles = channels // LANES
    index = lax.axis_index("rows")
    z, y, core = index // 4, (index // 2) % 2, index % 2
    idx = jnp.stack([z, y, core]).astype(jnp.int32)
    bias_row, gain_row = depth_bias.reshape(1, channels), norm_gain.reshape(1, channels)
    shift_row, scale_row = norm_shift.reshape(1, channels), layer_scale.reshape(1, channels)
    up_bias_row = up_bias.reshape(1, hidden_dev)

    cot_shard = cotangent.reshape(16, channels)
    planes, across = gather_chips(features)
    gain_dot, shift_dot, kern, own_shard = call(
        fold_kernel,
        1.5,
        10,
        (
            shape((8, hidden_dev), F32),
            shape((8, hidden_dev), F32),
            shape(depth_kernel.shape, F32),
            shape(features.shape, BF16),
        ),
        (gain_row, shift_row, up_weight, depth_kernel, features),
        scalars=0,
    )
    planes = [own_shard] + planes[1:]
    picks = [(2 * (1 - core) + half + 1 - z) % 4 for half in range(2)]
    chosen = [
        jnp.stack([lax.select_n(pick, *pieces) for pick in picks]) for pieces in (planes, across)
    ]
    with jax.named_scope("feat_core"):
        feat_came = [send(pieces, C_PAIRS) for pieces in chosen]
    with jax.named_scope("cot_y"):
        cot_pair = jnp.stack([cot_shard, send(cot_shard, Y_PAIRS)])
    with jax.named_scope("cot_z"):
        cot_late = after(cot_pair, tuple(planes[1:]))
        ahead, behind = send(cot_late, z_pairs(1)), send(cot_late, z_pairs(3))
        cot_planes = [cot_pair, ahead, send(ahead, z_pairs(1)), behind]
    half_tiles = tiles // 2
    turn = VMEM((4, 16, LANES), F32)
    square = VMEM((128, LANES), F32)
    conv_args = (*planes, *across, *feat_came, kern, bias_row)
    feats_low, conv_low, total_low = call(
        conv_kernel,
        8.0,
        12,
        (
            shape((half_tiles, 4, 48, LANES), F32),
            shape((half_tiles, 128, LANES), F32),
            shape((128, LANES), F32),
        ),
        (after(idx, (cot_planes[1], cot_planes[3])), *conv_args),
        (turn,),
    )
    normed, f_slice, u_slice, inv_slice = call(
        conv_norm_kernel,
        8.0,
        12,
        (
            shape((128, channels), BF16),
            shape((3, 4, 48, LANES), F32),
            shape((3, 128, LANES), F32),
            shape((128, LANES), F32),
        ),
        (
            idx, *conv_args, gain_row, shift_row,
            feats_low, conv_low, total_low,
        ),
        (
            VMEM((half_tiles, 4, 48, LANES), F32),
            VMEM((half_tiles, 128, LANES), F32),
            turn,
            square,
            square,
            square,
        ),
    )
    with jax.named_scope("cot_core"):
        cot_came = [send(after(plane, inv_slice), C_PAIRS) for plane in cot_planes]
    normed_other = send(normed, C_PAIRS)
    cot_all, cot_slice = call(
        cot_kernel,
        1.5,
        8,
        (shape((256, channels), BF16), shape((3, 128, LANES), F32)),
        (idx, *cot_planes, *cot_came, scale_row),
    )
    hid_grad = call(
        hid_kernel, 1.5, 8, shape((256, hidden_dev), F32), (cot_all, down_weight), scalars=0
    )
    halves = [
        call(
            functools.partial(act_kernel, half),
            1.7,
            12,
            (
                shape((128, hidden_dev), BF16),
                shape((128, hidden_dev), BF16),
                shape((1, hidden_dev), F32),
                shape((16, LANES), F32),
            ),
            (value, up_weight, up_bias_row, hid_grad, gain_dot, shift_dot),
            scalars=0,
        )
        for half, value in enumerate((normed, normed_other))
    ]
    hidden = [part[0] for part in halves]
    act_grad = [part[1] for part in halves]
    sums = [part[3] for part in halves]

    arrived, came_at, keep_at, across_at = {}, {}, {}, {}
    for pair in ((2, 3), (1, 0)):
        keep, away = call(
            functools.partial(norm_grad_kernel, pair),
            1.6,
            10,
            (shape((2, 2, 144, 384), F32), shape((2, 2, 144, 384), BF16)),
            (idx, *act_grad, up_weight, *sums),
        )
        came = send(away, C_PAIRS)
        for at, step in enumerate(pair):
            came_at[step], keep_at[step] = came[at].astype(F32), keep[at]
            across_at[step] = send((keep[at, 1] + came_at[step][1]).astype(BF16), Y_PAIRS)
    cots = (cot_all, cot_all)
    down_low = half_gradient(0, after(tuple(hidden), came), cots, 128)
    for step in (2, 3, 1, 0):
        total = keep_at[step][0] + came_at[step][0]
        if step == 1:
            total, down_low = lax.optimization_barrier((total, down_low))
        total = total + across_at[step].astype(F32)
        if step:
            total = send(total.astype(BF16), flipped(z_pairs(step)))
        arrived[step] = total
    down_grad = half_gradient(1, after(tuple(hidden), across_at[0]), cots, 128, down_low)
    late_idx, down_grad = lax.optimization_barrier((idx, down_grad))
    ig_keep, core_msg, small_keep = call(
        conv_back_kernel,
        2.2,
        12,
        (shape((4, 16, 384), BF16), shape((6, 16, 384), BF16), shape((2, 16, 384), F32)),
        (
            late_idx, arrived[0], arrived[1], arrived[2], arrived[3], f_slice, u_slice, inv_slice,
            gain_row, kern, cot_slice,
        ),
        (
            VMEM((3, 4, 48, LANES), F32),
            VMEM((3, 128, LANES), F32),
            VMEM((3, 128, LANES), F32),
            VMEM((64, 384), F32),
        ),
    )
    core_msg = send(core_msg, C_PAIRS)
    msgs = call(
        route_kernel,
        0.5,
        4,
        tuple(shape((4, 16, 384), BF16) for _ in range(4)),
        (idx, ig_keep, core_msg, small_keep),
    )
    msgs = [msgs[0]] + [send(msgs[step], flipped(z_pairs(step))) for step in (1, 2, 3)]
    up_low = half_gradient(0, after((normed, normed_other), msgs[3]), act_grad, 512)
    msgs, up_low = lax.optimization_barrier((msgs, up_low))
    came = send(jnp.stack([msg[1:4] for msg in msgs]), Y_PAIRS)
    core_a = send(jnp.stack([msg[2:4] for msg in msgs]), C_PAIRS)
    up_grad = half_gradient(1, after((normed, normed_other), core_a), act_grad, 512, up_low)
    late, up_grad = lax.optimization_barrier((came[:, 1:3], up_grad))
    core_b = send(late, C_PAIRS)
    row = shape((1, channels), F32)
    tokens, kernel_grad, gain_grad, shift_grad, depth_bias_grad = call(
        place_kernel,
        0.8,
        8,
        (shape((4, 4, channels), BF16), shape((7, 7, channels), F32), row, row, row),
        (idx, *msgs, came, core_a, core_b),
    )
    return (
        tokens,
        up_grad,
        (halves[0][2] + halves[1][2]).reshape(hidden_dev),
        down_grad,
        kernel_grad,
        depth_bias_grad.reshape(channels),
        gain_grad.reshape(channels),
        shift_grad.reshape(channels),
    )


def on_device(features, *rest):
    rows_dev, cols, channels = features.shape
    fits = lax.axis_size("rows") == 16 and rows_dev == 4 and cols == 4 and channels == 3072
    return (sliced_device if fits else generic_device)(features, *rest)


def solution(mesh):
    in_specs = (
        P(("groups", "rows"), None, None),
        P(("groups", "rows"), None, None),
        P(),
        P(),
        P(),
        P(),
        P(None, "rows"),
        P("rows"),
        P("rows", None),
        P(),
    )
    out_specs = (
        P(("groups", "rows"), None, None),
        P("groups", "rows"),
        P(("groups", "rows")),
        P(("groups", "rows"), None),
        P("groups", None, None),
        P("groups"),
        P("groups"),
        P("groups"),
    )
    return jax.shard_map(
        on_device, mesh=mesh, in_specs=in_specs, out_specs=out_specs, check_vma=False
    )
```

```python
import functools

import jax
import jax.numpy as jnp
from jax import lax
from jax.experimental import pallas as pl
from jax.experimental.pallas import tpu as pltpu
from jax.sharding import PartitionSpec as P

IMG_ROWS = 32
BF16 = jnp.bfloat16
F32 = jnp.float32


def stages_of(count):
    sizes = []
    chips = count // 2
    while chips % 4 == 0 and chips > 4:
        sizes.append(4)
        chips //= 4
    if chips > 1:
        sizes.append(chips)
    out = [(1, 2)]
    stride = 2
    for size in reversed(sizes):
        out.insert(0, (stride, size))
        stride *= size
    return out


def from_ahead(count, stride, size, step):
    pairs = []
    for i in range(count):
        digit = (i // stride) % size
        src = i + ((digit + step) % size - digit) * stride
        pairs.append((src, i))
    return pairs


def send(value, pairs):
    return lax.ppermute(value, "rows", pairs)


def gather_stage(value, count, stride, size):
    parts = [value]
    for step in range(1, size):
        parts.append(send(value, from_ahead(count, stride, size, step)))
    return jnp.stack(parts)


def scatter_stage(value, count, stride, size):
    total = value[0].astype(F32)
    for step in range(1, size):
        back = [(dst, src) for src, dst in from_ahead(count, stride, size, step)]
        total = total + send(value[step], back).astype(F32)
    return total


def gelu_parts(pre_act):
    cdf = 0.5 * (1.0 + jax.scipy.special.erf(pre_act * 0.7071067811865476))
    slope = cdf + pre_act * jnp.exp(-0.5 * pre_act * pre_act) * 0.3989422804014327
    return pre_act * cdf, slope


def contract(left, right, left_dim, right_dim):
    return lax.dot_general(
        left, right, (((left_dim,), (right_dim,)), ((), ())), preferred_element_type=F32
    )


def extended(cells, width, fwd, bwd):
    head = lax.slice_in_dim(cells, 0, width, axis=0)
    tail = lax.slice_in_dim(cells, cells.shape[0] - width, cells.shape[0], axis=0)
    return jnp.concatenate([send(tail, fwd), cells, send(head, bwd)], axis=0)


def generic_device(
    features,
    cotangent,
    depth_kernel,
    depth_bias,
    norm_gain,
    norm_shift,
    up_weight,
    up_bias,
    down_weight,
    layer_scale,
):
    rows_dev, cols, channels = features.shape
    count = lax.axis_size("rows")
    stages = stages_of(count)
    shard = rows_dev * cols
    half_image = IMG_ROWS // 2
    crossing = [
        (i, (i + 1) % count)
        for i in range(count)
        if ((i + 1) * rows_dev - half_image) % IMG_ROWS != 0
    ]
    fwd = crossing
    bwd = [(b, a) for a, b in crossing]
    pieces = 2
    width = channels // pieces

    def gather(value):
        outs = []
        for p in range(pieces):
            part = value[:, p * width : (p + 1) * width]
            for stride, size in stages:
                part = gather_stage(part, count, stride, size)
            outs.append(part.reshape(shard * count, width))
        return outs

    near = extended(features, 3, fwd, bwd).astype(F32)
    cot_scaled = (
        (cotangent.astype(F32) * layer_scale).astype(BF16).reshape(shard, channels)
    )
    cot_all = gather(cot_scaled)
    padded = jnp.pad(near, ((0, 0), (3, 3), (0, 0)))
    conv_out = jnp.zeros((rows_dev, cols, channels), F32)
    for i in range(7):
        for j in range(7):
            conv_out = conv_out + depth_kernel[i, j] * padded[i : i + rows_dev, j : j + cols]
    conv_out = conv_out + depth_bias
    row_mean = jnp.mean(conv_out, axis=-1, keepdims=True)
    centred = conv_out - row_mean
    inv_std = lax.rsqrt(jnp.mean(centred * centred, axis=-1, keepdims=True) + 1e-06)
    unit_norm = centred * inv_std
    normed = (unit_norm * norm_gain + norm_shift).astype(BF16).reshape(shard, channels)
    normed_all = gather(normed)

    hid_grad = sum(
        contract(cot_all[p], down_weight[:, p * width : (p + 1) * width], 1, 1)
        for p in range(pieces)
    )
    pre_act = up_bias + sum(
        contract(normed_all[p], up_weight[p * width : (p + 1) * width], 1, 0)
        for p in range(pieces)
    )
    value, slope = gelu_parts(pre_act)
    hidden = value.astype(BF16)
    act_grad = (hid_grad * slope).astype(BF16)

    norm_parts = []
    for p in range(pieces):
        part = contract(act_grad, up_weight[p * width : (p + 1) * width], 1, 1).astype(BF16)
        lead = [size for _, size in reversed(stages)]
        part = part.reshape(*lead, shard, width)
        for stride, size in reversed(stages):
            part = scatter_stage(part, count, stride, size)
            if stride != stages[0][0]:
                part = part.astype(BF16)
        norm_parts.append(part)
    norm_grad = jnp.concatenate(norm_parts, axis=-1).reshape(rows_dev, cols, channels)

    up_bias_grad = jnp.sum(act_grad.astype(F32), axis=0)
    down_grad = jnp.concatenate([contract(hidden, c, 0, 0) for c in cot_all], axis=1)
    up_grad = jnp.concatenate([contract(n, act_grad, 0, 0) for n in normed_all], axis=0)

    gain_part = jnp.sum(norm_grad * unit_norm, axis=(0, 1))
    shift_part = jnp.sum(norm_grad, axis=(0, 1))
    scaled = norm_grad * norm_gain
    conv_grad = inv_std * (
        scaled
        - jnp.mean(scaled, axis=-1, keepdims=True)
        - unit_norm * jnp.mean(scaled * unit_norm, axis=-1, keepdims=True)
    )
    bias_part = jnp.sum(conv_grad, axis=(0, 1))
    rows_out = [
        jnp.sum(conv_grad * padded[i : i + rows_dev, j : j + cols], axis=(0, 1))
        for i in range(7)
        for j in range(7)
    ]
    near_grad = extended(conv_grad.astype(BF16), 3, fwd, bwd).astype(F32)
    grad_padded = jnp.pad(near_grad, ((0, 0), (3, 3), (0, 0)))

    chips = count // 2
    per = -(-52 // chips)
    small = jnp.stack(rows_out + [gain_part, shift_part, bias_part])
    small = jnp.pad(small, ((0, per * chips - 52), (0, 0)))
    half = channels // 2
    small = small.reshape(chips, per, 2, half).transpose(2, 0, 1, 3)
    core = lax.axis_index("rows") % 2
    swapped = jnp.where(core == 0, small, small[::-1])
    swapped = swapped.astype(BF16)
    mine = swapped[0].astype(F32) + send(
        swapped[1], from_ahead(count, 1, 2, 1)
    ).astype(F32)
    mine = mine.astype(BF16)
    chip = lax.axis_index("rows") // 2
    ahead = jnp.roll(mine, -chip, axis=0)
    total = ahead[0].astype(F32)
    for step in range(1, chips):
        back = [(dst, src) for src, dst in from_ahead(count, 2, chips, step)]
        total = total + send(ahead[step], back).astype(F32)
    total = total.astype(BF16)
    every = [total] + [
        send(total, from_ahead(count, 2, chips, step)) for step in range(1, chips)
    ]
    every = jnp.roll(jnp.stack(every), chip, axis=0)
    other = send(every, from_ahead(count, 1, 2, 1))
    both = jnp.where(
        core == 0,
        jnp.concatenate([every, other], axis=-1),
        jnp.concatenate([other, every], axis=-1),
    )
    both = both.reshape(per * chips, channels).astype(F32)
    kernel_grad = both[:49].reshape(7, 7, channels)
    gain_grad, shift_grad, depth_bias_grad = both[49], both[50], both[51]

    back_term = jnp.zeros((rows_dev, cols, channels), F32)
    for i in range(7):
        for j in range(7):
            back_term = back_term + depth_kernel[i, j] * grad_padded[
                6 - i : 6 - i + rows_dev, 6 - j : 6 - j + cols
            ]
    input_grad = (cotangent.astype(F32) + back_term).astype(BF16)
    return (
        input_grad,
        up_grad,
        up_bias_grad,
        down_grad,
        kernel_grad,
        depth_bias_grad,
        gain_grad,
        shift_grad,
    )


LANES = 128
VMEM = pltpu.VMEM
VSPEC = pl.BlockSpec(memory_space=pltpu.VMEM)
SSPEC = pl.BlockSpec(memory_space=pltpu.SMEM)
EXACT = lax.Precision.HIGHEST
MIB = 1024 * 1024


def z_pairs(step):
    return from_ahead(16, 4, 4, step)


def flipped(pairs):
    return [(dst, src) for src, dst in pairs]


Y_PAIRS = from_ahead(16, 2, 2, 1)
C_PAIRS = from_ahead(16, 1, 2, 1)


def after(value, other):
    return lax.optimization_barrier((value, other))[0]


def gather_chips(shard):
    with jax.named_scope("feat_z"):
        planes = [shard] + [send(shard, z_pairs(step)) for step in (1, 2, 3)]
    with jax.named_scope("feat_y"):
        return planes, [send(plane, Y_PAIRS) for plane in planes]


def lane_tile(tile):
    return pl.ds(pl.multiple_of(tile * LANES, LANES), LANES)


def sixteen(block):
    return pl.ds(pl.multiple_of(block * 16, 16), 16)


def place_and_convolve(idx, pieces, came, kern, bias, feats, conv, turn, total, first_tile):
    z, y, core = idx[0], idx[1], idx[2]
    tiles = feats.shape[0]
    edge = jnp.zeros((tiles, 4, 8, LANES), F32)
    feats[:, :, 0:8, :] = edge
    feats[:, :, 40:48, :] = edge

    def place(piece, row):
        for tile in range(tiles):
            lanes = slice((first_tile + tile) * LANES, (first_tile + tile + 1) * LANES)
            for r in range(4):
                turn[tile % 4, 4 * r : 4 * r + 4, :] = piece[r, :, lanes].astype(F32)
            for col in range(4):
                feats[tile, col, pl.ds(8 + row, 4), :] = turn[
                    tile % 4, pl.ds(col, 4, stride=4), :
                ]

    for yr in range(2):
        for step in range(4):
            at = (z + step + 3) % 4

            @pl.when(at // 2 == core)
            def _():
                place(pieces[4 * yr + step], 16 * (at % 2) + 8 * ((y + yr) % 2) + 4 * core)

        for half in range(2):
            place(came[yr].at[half], 16 * half + 8 * ((y + yr) % 2) + 4 * (1 - core))

    def conv_tile(tile, carry):
        lanes = lane_tile(first_tile + tile)
        for part in range(2):
            acc = [jnp.broadcast_to(bias[0:1, lanes], (16, LANES))] * 4
            for i in range(7):
                for src in range(4):
                    rows = feats[tile, src, pl.ds(5 + 16 * part + i, 16), :]
                    for col in range(4):
                        j = src - col + 3
                        acc[col] = acc[col] + kern[i, j : j + 1, lanes] * rows
            for col in range(4):
                at = pl.ds(64 * part + col, 16, stride=4)
                conv[tile, at, :] = acc[col]
        total[...] = total[...] + conv[tile]
        return carry

    lax.fori_loop(0, tiles, conv_tile, 0)


def conv_kernel(idx, *refs):
    kern, bias, feats, conv, total, turn = refs[10:]
    total[...] = jnp.zeros_like(total)
    place_and_convolve(
        idx, refs[:8], refs[8:10], kern, bias, feats, conv, turn, total, 0
    )


def conv_norm_kernel(idx, *refs):
    kern, bias, gain, shift, feats_low, conv_low, total_low = refs[10:17]
    normed, f_slice, u_slice, inv_slice = refs[17:21]
    feats, conv, turn, total, mean_ref, inv_ref = refs[21:]
    tiles = feats.shape[0]
    channels = 2 * tiles * LANES
    total[...] = total_low[...]
    place_and_convolve(
        idx, refs[:8], refs[8:10], kern, bias, feats, conv, turn, total, tiles
    )
    mean = jnp.sum(total[...], axis=-1, keepdims=True) / channels
    mean_ref[...] = jnp.broadcast_to(mean, mean_ref.shape)
    total[...] = jnp.zeros_like(total)
    halves = ((0, conv_low, feats_low), (tiles, conv, feats))

    def square_tile(tile, carry):
        low, high = conv_low[tile] - mean_ref[...], conv[tile] - mean_ref[...]
        total[...] = total[...] + (low * low + high * high)
        return carry

    lax.fori_loop(0, tiles, square_tile, 0)
    spread = jnp.sum(total[...], axis=-1, keepdims=True) / channels
    inv_ref[...] = jnp.broadcast_to(lax.rsqrt(spread + 1e-06), inv_ref.shape)

    def norm_tile(tile, carry):
        for start, values, _ in halves:
            lanes = lane_tile(start + tile)
            unit = (values[tile] - mean_ref[...]) * inv_ref[...]
            normed[:, lanes] = (unit * gain[0:1, lanes] + shift[0:1, lanes]).astype(BF16)
        return carry

    lax.fori_loop(0, tiles, norm_tile, 0)
    chip = idx[0] * 2 + idx[1]
    inv_slice[...] = inv_ref[...]
    for start, values, padded in halves:

        @pl.when((chip >= 4) == (start > 0))
        def _():
            for k in range(3):
                tile = (chip % 4) * 3 + k
                u_slice[k] = (values[tile] - mean_ref[...]) * inv_ref[...]
                f_slice[k] = padded[tile]


def cot_kernel(idx, *refs):
    layer_scale, cot_all, cot_slice = refs[8:]
    z, y, core = idx[0], idx[1], idx[2]
    chip = z * 2 + y
    own = lane_tile(chip * 3), lane_tile(chip * 3 + 1), lane_tile(chip * 3 + 2)
    for yr in range(2):
        for cr in range(2):
            for step in range(4):
                piece = refs[4 * cr + step].at[yr]
                at = (z + step + 3) % 4
                away = (at // 2 + core) % 2
                block = 4 * (at % 2) + 2 * ((y + yr) % 2) + (core + cr) % 2
                scaled = piece[...].astype(F32) * layer_scale[...]
                cot_all[sixteen(8 * away + block), :] = scaled.astype(BF16)

                @pl.when(away == 0)
                def _():
                    for k in range(3):
                        cot_slice[k, sixteen(block), :] = piece[:, own[k]].astype(F32)


def fold_kernel(gain, shift, weight, kern, shard, gain_dot, shift_dot, kern_out, shard_out):
    kern_out[...] = kern[...]
    shard_out[...] = shard[...]
    place = lax.broadcasted_iota(jnp.int32, (16, gain.shape[1]), 0)
    scale, offset = gain[...], shift[...]
    scale_hi = scale.astype(BF16).astype(F32)
    offset_hi = offset.astype(BF16).astype(F32)
    both = jnp.where(place == 0, scale_hi, 0.0)
    both = jnp.where(place == 1, scale - scale_hi, both)
    both = jnp.where(place == 2, offset_hi, both)
    both = jnp.where(place == 3, offset - offset_hi, both)
    product = jnp.dot(both.astype(BF16), weight[...], preferred_element_type=F32)
    gain_dot[...] = jnp.broadcast_to(product[0:1] + product[1:2], gain_dot.shape)
    shift_dot[...] = jnp.broadcast_to(product[2:3] + product[3:4], shift_dot.shape)


def up_kernel(normed, weight, up_bias, shift_dot, hidden, slope, centred):
    tile = 256
    for start in range(0, hidden.shape[1], tile):
        at = slice(start, start + tile)
        plain = jnp.dot(normed[...], weight[:, at], preferred_element_type=F32)
        pre_act = plain + up_bias[0:1, at]
        cdf = 0.5 * (1.0 + lax.erf(pre_act * 0.7071067811865476))
        hidden[:, at] = (pre_act * cdf).astype(BF16)
        slope[:, at] = cdf + pre_act * jnp.exp(-0.5 * pre_act * pre_act) * 0.3989422804014327
        centred[:, at] = plain - shift_dot[0:1, at]


def act_kernel(
    cot_all, weight, gain_dot, slope_own, slope_other, centred_own, centred_other,
    act_own, act_other, bias_grad, sums_own, sums_other,
):
    tile = 256
    halves = (
        (0, slope_own, centred_own, act_own, sums_own),
        (128, slope_other, centred_other, act_other, sums_other),
    )
    parts = [jnp.zeros((128, LANES), F32) for _ in range(4)]
    for start in range(0, act_own.shape[1], tile):
        at = slice(start, start + tile)
        hid_grad = contract(cot_all[...], weight[at, :], 1, 1)
        column = jnp.zeros((1, tile), F32)
        for half, (row, slope, centred, act_grad, _) in enumerate(halves):
            act = (hid_grad[row : row + 128] * slope[:, at]).astype(BF16)
            act_grad[:, at] = act
            act = act.astype(F32)
            column = column + jnp.sum(act, axis=0, keepdims=True)
            by_gain = act * gain_dot[0:1, at]
            by_unit = act * centred[:, at]
            for lane in range(0, tile, LANES):
                parts[2 * half] = parts[2 * half] + by_gain[:, lane : lane + LANES]
                parts[2 * half + 1] = parts[2 * half + 1] + by_unit[:, lane : lane + LANES]
        bias_grad[0:1, at] = column
    ones = jnp.ones((8, LANES), F32)
    for half, (_, _, _, _, sums) in enumerate(halves):
        for which in range(2):
            sums[8 * which : 8 * which + 8, :] = lax.dot_general(
                ones, parts[2 * half + which], (((1,), (1,)), ((), ())),
                precision=EXACT, preferred_element_type=F32,
            )


def norm_grad_kernel(steps, idx, act_own, act_other, weight, sums_own, sums_other, keep, away):
    both = jnp.concatenate([act_other[...], act_own[...]], axis=0)
    for at, step in enumerate(steps):
        for yr in range(2):
            chip = 2 * ((idx[0] + step) % 4) + (idx[1] + yr) % 2
            rows = weight[pl.ds(pl.multiple_of(chip * 384, 128), 384), :]
            product = contract(both, rows, 1, 1)
            for ref, part, sums in ((away, 0, sums_other), (keep, 128, sums_own)):
                ref[at, yr, 0:128, :] = product[part : part + 128].astype(ref.dtype)
                ref[at, yr, 128:144, 0:128] = sums[...].astype(ref.dtype)
                ref[at, yr, 128:144, 128:384] = jnp.zeros((16, 256), ref.dtype)


def grad_kernel(left_own, left_other, right_own, right_other, *rest):
    left = jnp.concatenate([left_own[...], left_other[...]], axis=0).T
    right = jnp.concatenate([right_own[...], right_other[...]], axis=0)
    rest[-1][...] = contract(left, right, 1, 0)


def conv_back_kernel(
    idx, own, near_1, near_2, near_3, f_slice, u_slice, inv_slice, gain, kern, cot_slice,
    ig_keep, core_msg, small_keep, cg, turn, back, small,
):
    chip, y, core = idx[0] * 2 + idx[1], idx[1], idx[2]
    channels = gain.shape[1]

    def summed(rows, lanes):
        return (
            own[rows, lanes]
            + near_1[rows, lanes].astype(F32)
            + near_2[rows, lanes].astype(F32)
            + near_3[rows, lanes].astype(F32)
        )

    sums = summed(slice(128, 144), slice(0, 128))
    place = lax.broadcasted_iota(jnp.int32, (16, LANES), 0)

    def per_token(row):
        pick = jnp.where(place == row, 1.0 / channels, 0.0).astype(F32)
        return lax.dot_general(
            sums, pick, (((0,), (0,)), ((), ())), precision=EXACT, preferred_element_type=F32
        )

    mean_1, mean_2 = per_token(0), per_token(8)
    cg[:, :, 0:8, :] = jnp.zeros((3, 4, 8, LANES), F32)
    cg[:, :, 40:48, :] = jnp.zeros((3, 4, 8, LANES), F32)
    small[...] = jnp.zeros_like(small)
    for k in range(3):
        lanes = slice(k * LANES, (k + 1) * LANES)
        wide = lane_tile(chip * 3 + k)
        norm_grad = summed(slice(0, 128), lanes)
        unit = u_slice[k]
        scaled = norm_grad * gain[0:1, wide]
        grad = inv_slice[...] * (scaled - mean_1 - unit * mean_2)
        turn[k] = grad
        for col in range(4):
            cg[k, col, 8:40, :] = turn[k, pl.ds(col, 32, stride=4), :]
        small[56:57, lanes] = jnp.sum(norm_grad * unit, axis=0, keepdims=True)
        small[57:58, lanes] = jnp.sum(norm_grad, axis=0, keepdims=True)
        small[58:59, lanes] = jnp.sum(grad, axis=0, keepdims=True)
        for i in range(7):
            acc = [None] * 7
            for src in range(4):
                rows = f_slice[k, src, 5 + i : 37 + i, :]
                for col in range(4):
                    j = src - col + 3
                    term = cg[k, col, 8:40, :] * rows
                    acc[j] = term if acc[j] is None else acc[j] + term
            for j in range(7):
                small[8 * i + j : 8 * i + j + 1, lanes] = jnp.sum(acc[j], axis=0, keepdims=True)
        for part in range(2):
            acc = [cot_slice[k, pl.ds(64 * part + col, 16, stride=4), :] for col in range(4)]
            for i in range(7):
                for src in range(4):
                    start = 11 + 16 * part - i
                    rows = cg[k, src, start : start + 16, :]
                    for col in range(4):
                        j = col - src + 3
                        acc[col] = acc[col] + kern[i, j : j + 1, wide] * rows
            for col in range(4):
                back[k, pl.ds(64 * part + col, 16, stride=4), :] = acc[col]
        for half in range(2):
            for yr in range(2):
                for cr in range(2):
                    block = 4 * half + 2 * ((y + yr) % 2) + (core + cr) % 2
                    ref = core_msg if cr else ig_keep
                    ref[2 * half + yr, :, lanes] = back[k, sixteen(block), :].astype(BF16)
    for part in range(2):
        core_msg[4 + part] = small[sixteen(2 * (1 - core) + part), :].astype(BF16)
        small_keep[part] = small[sixteen(2 * core + part), :]


def route_kernel(idx, ig_keep, core_msg, small_keep, *msgs):
    z, core = idx[0], idx[2]
    total = [
        (small_keep[part] + core_msg[4 + part].astype(F32)).astype(BF16) for part in range(2)
    ]
    for step in range(4):
        at = (z + step + 3) % 4
        image, half = at // 2, at % 2
        for yr in range(2):
            kept, came = ig_keep[2 * half + yr], core_msg[2 * half + yr]
            msgs[step][yr] = jnp.where(image == core, kept, came)
        for part in range(2):
            msgs[step][2 + part] = total[part]


def place_kernel(idx, *refs):
    msgs, came, across_core = refs[:4], refs[4], refs[5]
    tokens, kernel_grad, gain_grad, shift_grad, bias_grad = refs[6:]
    z, y, core = idx[0], idx[1], idx[2]
    for step in range(4):
        plane = (z + 4 - step) % 4
        for yr in range(2):
            chip = plane * 2 + (y + yr) % 2
            lanes = pl.ds(pl.multiple_of(chip * 384, 128), 384)
            block = (came[step, 0] if yr else msgs[step][0]).astype(F32)
            for row in range(4):
                tokens[row, :, lanes] = block[4 * row : 4 * row + 4].astype(BF16)
            for part in range(2):
                mine = (came[step, 1 + part] if yr else msgs[step][2 + part]).astype(F32)
                other = across_core[yr, step, part].astype(F32)
                low = jnp.where(core == 0, mine, other)
                high = jnp.where(core == 0, other, mine)
                for sub in range(2):
                    at = 2 * part + sub
                    rows = slice(8 * sub, 8 * sub + 7)
                    kernel_grad[at, :, lanes] = low[rows]
                    if at < 3:
                        kernel_grad[4 + at, :, lanes] = high[rows]
                    else:
                        gain_grad[0:1, lanes] = high[8:9]
                        shift_grad[0:1, lanes] = high[9:10]
                        bias_grad[0:1, lanes] = high[10:11]


def shape(dims, dtype):
    return jax.ShapeDtypeStruct(dims, dtype)


def call(kernel, micros, room, out_shape, inputs, scratch=(), scalars=1):
    return pl.pallas_call(
        kernel,
        out_shape=out_shape,
        in_specs=[SSPEC] * scalars + [VSPEC] * (len(inputs) - scalars),
        out_specs=jax.tree.map(lambda _: VSPEC, out_shape),
        scratch_shapes=list(scratch),
        compiler_params=pltpu.CompilerParams(vmem_limit_bytes=room * MIB),
        cost_estimate=cost(micros),
    )(*inputs)


def cost(micros):
    return pl.CostEstimate(
        flops=int(micros * 1.1e9), bytes_accessed=int(micros * 3.4e6), transcendentals=0
    )


def half_gradient(part, left, right, tile, so_far=None):
    rows, cols = left[0].shape[1], right[0].shape[1]
    steps = rows // 2 // tile
    left_spec = pl.BlockSpec((128, tile), lambda m: (0, part * steps + m))
    right_spec = pl.BlockSpec((128, cols), lambda m: (0, 0))
    whole = right[1] is right[0]
    other_spec = pl.BlockSpec((128, cols), lambda m: (1, 0)) if whole else right_spec
    extra = () if so_far is None else (so_far,)
    return pl.pallas_call(
        grad_kernel,
        grid=(steps,),
        out_shape=shape((rows, cols), F32),
        in_specs=[left_spec, left_spec, right_spec, other_spec]
        + [pl.BlockSpec(memory_space=pl.ANY)] * len(extra),
        out_specs=pl.BlockSpec((tile, cols), lambda m: (part * steps + m, 0)),
        input_output_aliases={4: 0} if extra else {},
        compiler_params=pltpu.CompilerParams(vmem_limit_bytes=16 * MIB),
        cost_estimate=cost(2.5),
    )(*left, *right, *extra)


def sliced_device(
    features,
    cotangent,
    depth_kernel,
    depth_bias,
    norm_gain,
    norm_shift,
    up_weight,
    up_bias,
    down_weight,
    layer_scale,
):
    channels, hidden_dev = up_weight.shape
    tiles = channels // LANES
    index = lax.axis_index("rows")
    z, y, core = index // 4, (index // 2) % 2, index % 2
    idx = jnp.stack([z, y, core]).astype(jnp.int32)
    bias_row, gain_row = depth_bias.reshape(1, channels), norm_gain.reshape(1, channels)
    shift_row, scale_row = norm_shift.reshape(1, channels), layer_scale.reshape(1, channels)
    up_bias_row = up_bias.reshape(1, hidden_dev)

    cot_shard = cotangent.reshape(16, channels)
    planes, across = gather_chips(features)
    gain_dot, shift_dot, kern, own_shard = call(
        fold_kernel,
        1.5,
        10,
        (
            shape((8, hidden_dev), F32),
            shape((8, hidden_dev), F32),
            shape(depth_kernel.shape, F32),
            shape(features.shape, BF16),
        ),
        (gain_row, shift_row, up_weight, depth_kernel, features),
        scalars=0,
    )
    planes = [own_shard] + planes[1:]
    picks = [(2 * (1 - core) + half + 1 - z) % 4 for half in range(2)]
    chosen = [
        jnp.stack([lax.select_n(pick, *pieces) for pick in picks]) for pieces in (planes, across)
    ]
    with jax.named_scope("feat_core"):
        feat_came = [send(pieces, C_PAIRS) for pieces in chosen]
    with jax.named_scope("cot_y"):
        cot_pair = jnp.stack([cot_shard, send(cot_shard, Y_PAIRS)])
    with jax.named_scope("cot_z"):
        cot_late = after(cot_pair, tuple(planes[1:]))
        ahead, behind = send(cot_late, z_pairs(1)), send(cot_late, z_pairs(3))
        cot_planes = [cot_pair, ahead, send(ahead, z_pairs(1)), behind]
    half_tiles = tiles // 2
    turn = VMEM((4, 16, LANES), F32)
    square = VMEM((128, LANES), F32)
    conv_args = (*planes, *across, *feat_came, kern, bias_row)
    feats_low, conv_low, total_low = call(
        conv_kernel,
        8.0,
        12,
        (
            shape((half_tiles, 4, 48, LANES), F32),
            shape((half_tiles, 128, LANES), F32),
            shape((128, LANES), F32),
        ),
        (after(idx, (cot_planes[1], cot_planes[3])), *conv_args),
        (turn,),
    )
    normed, f_slice, u_slice, inv_slice = call(
        conv_norm_kernel,
        8.0,
        12,
        (
            shape((128, channels), BF16),
            shape((3, 4, 48, LANES), F32),
            shape((3, 128, LANES), F32),
            shape((128, LANES), F32),
        ),
        (
            idx, *conv_args, gain_row, shift_row,
            feats_low, conv_low, total_low,
        ),
        (
            VMEM((half_tiles, 4, 48, LANES), F32),
            VMEM((half_tiles, 128, LANES), F32),
            turn,
            square,
            square,
            square,
        ),
    )
    with jax.named_scope("cot_core"):
        cot_came = [send(after(plane, inv_slice), C_PAIRS) for plane in cot_planes]
    normed_other = send(after(normed, cot_planes[2]), C_PAIRS)
    half_f32 = shape((128, hidden_dev), F32)
    half_bf16 = shape((128, hidden_dev), BF16)
    ups = [
        call(
            up_kernel,
            0.1,
            12,
            (half_bf16, half_f32, half_f32),
            (value, up_weight, up_bias_row, shift_dot),
            scalars=0,
        )
        for value in (normed, normed_other)
    ]
    hidden, slope, centred = zip(*ups)
    cot_all, cot_slice = call(
        cot_kernel,
        1.5,
        8,
        (shape((256, channels), BF16), shape((3, 128, LANES), F32)),
        (after(idx, slope), *cot_planes, *cot_came, scale_row),
    )
    act_own, act_other, up_bias_grad, *sums = call(
        act_kernel,
        2.2,
        12,
        (
            half_bf16,
            half_bf16,
            shape((1, hidden_dev), F32),
            shape((16, LANES), F32),
            shape((16, LANES), F32),
        ),
        (cot_all, down_weight, gain_dot, *slope, *centred),
        scalars=0,
    )
    act_grad = (act_own, act_other)

    arrived, came_at, keep_at, across_at = {}, {}, {}, {}
    for pair in ((2, 3), (1, 0)):
        keep, away = call(
            functools.partial(norm_grad_kernel, pair),
            1.6,
            10,
            (shape((2, 2, 144, 384), F32), shape((2, 2, 144, 384), BF16)),
            (idx, *act_grad, up_weight, *sums),
        )
        came = send(away, C_PAIRS)
        for at, step in enumerate(pair):
            came_at[step], keep_at[step] = came[at].astype(F32), keep[at]
            across_at[step] = send((keep[at, 1] + came_at[step][1]).astype(BF16), Y_PAIRS)
    cots = (cot_all, cot_all)
    down_low = half_gradient(0, after(hidden, came), cots, 128)
    for step in (2, 3, 1, 0):
        total = keep_at[step][0] + came_at[step][0]
        if step == 1:
            total, down_low = lax.optimization_barrier((total, down_low))
        total = total + across_at[step].astype(F32)
        if step:
            total = send(total.astype(BF16), flipped(z_pairs(step)))
        arrived[step] = total
    down_grad = half_gradient(1, after(hidden, across_at[0]), cots, 128, down_low)
    late_idx, down_grad = lax.optimization_barrier((idx, down_grad))
    ig_keep, core_msg, small_keep = call(
        conv_back_kernel,
        2.2,
        12,
        (shape((4, 16, 384), BF16), shape((6, 16, 384), BF16), shape((2, 16, 384), F32)),
        (
            late_idx, arrived[0], arrived[1], arrived[2], arrived[3], f_slice, u_slice, inv_slice,
            gain_row, kern, cot_slice,
        ),
        (
            VMEM((3, 4, 48, LANES), F32),
            VMEM((3, 128, LANES), F32),
            VMEM((3, 128, LANES), F32),
            VMEM((64, 384), F32),
        ),
    )
    core_msg = send(core_msg, C_PAIRS)
    msgs = call(
        route_kernel,
        0.5,
        4,
        tuple(shape((4, 16, 384), BF16) for _ in range(4)),
        (idx, ig_keep, core_msg, small_keep),
    )
    msgs = [msgs[0]] + [send(msgs[step], flipped(z_pairs(step))) for step in (1, 2, 3)]
    up_low = half_gradient(0, after((normed, normed_other), msgs[3]), act_grad, 512)
    msgs, up_low = lax.optimization_barrier((msgs, up_low))
    came = send(jnp.stack([msg[1:4] for msg in msgs]), Y_PAIRS)
    up_grad = half_gradient(1, after((normed, normed_other), msgs[1]), act_grad, 512, up_low)
    near = jnp.stack([msg[2:4] for msg in msgs])
    both, up_grad = lax.optimization_barrier((jnp.stack([near, came[:, 1:3]]), up_grad))
    across_core = send(both, C_PAIRS)
    row = shape((1, channels), F32)
    tokens, kernel_grad, gain_grad, shift_grad, depth_bias_grad = call(
        place_kernel,
        0.8,
        8,
        (shape((4, 4, channels), BF16), shape((7, 7, channels), F32), row, row, row),
        (idx, *msgs, came, across_core),
    )
    return (
        tokens,
        up_grad,
        up_bias_grad.reshape(hidden_dev),
        down_grad,
        kernel_grad,
        depth_bias_grad.reshape(channels),
        gain_grad.reshape(channels),
        shift_grad.reshape(channels),
    )


def on_device(features, *rest):
    rows_dev, cols, channels = features.shape
    fits = lax.axis_size("rows") == 16 and rows_dev == 4 and cols == 4 and channels == 3072
    return (sliced_device if fits else generic_device)(features, *rest)


def solution(mesh):
    in_specs = (
        P(("groups", "rows"), None, None),
        P(("groups", "rows"), None, None),
        P(),
        P(),
        P(),
        P(),
        P(None, "rows"),
        P("rows"),
        P("rows", None),
        P(),
    )
    out_specs = (
        P(("groups", "rows"), None, None),
        P("groups", "rows"),
        P(("groups", "rows")),
        P(("groups", "rows"), None),
        P("groups", None, None),
        P("groups"),
        P("groups"),
        P("groups"),
    )
    return jax.shard_map(
        on_device, mesh=mesh, in_specs=in_specs, out_specs=out_specs, check_vma=False
    )
```

```python
import functools

import jax
import jax.numpy as jnp
from jax import lax
from jax.experimental import pallas as pl
from jax.experimental.pallas import tpu as pltpu
from jax.sharding import PartitionSpec as P

IMG_ROWS = 32
BF16 = jnp.bfloat16
F32 = jnp.float32


def stages_of(count):
    sizes = []
    chips = count // 2
    while chips % 4 == 0 and chips > 4:
        sizes.append(4)
        chips //= 4
    if chips > 1:
        sizes.append(chips)
    out = [(1, 2)]
    stride = 2
    for size in reversed(sizes):
        out.insert(0, (stride, size))
        stride *= size
    return out


def from_ahead(count, stride, size, step):
    pairs = []
    for i in range(count):
        digit = (i // stride) % size
        src = i + ((digit + step) % size - digit) * stride
        pairs.append((src, i))
    return pairs


def send(value, pairs):
    return lax.ppermute(value, "rows", pairs)


def gather_stage(value, count, stride, size):
    parts = [value]
    for step in range(1, size):
        parts.append(send(value, from_ahead(count, stride, size, step)))
    return jnp.stack(parts)


def scatter_stage(value, count, stride, size):
    total = value[0].astype(F32)
    for step in range(1, size):
        back = [(dst, src) for src, dst in from_ahead(count, stride, size, step)]
        total = total + send(value[step], back).astype(F32)
    return total


def gelu_parts(pre_act):
    cdf = 0.5 * (1.0 + jax.scipy.special.erf(pre_act * 0.7071067811865476))
    slope = cdf + pre_act * jnp.exp(-0.5 * pre_act * pre_act) * 0.3989422804014327
    return pre_act * cdf, slope


def contract(left, right, left_dim, right_dim):
    return lax.dot_general(
        left, right, (((left_dim,), (right_dim,)), ((), ())), preferred_element_type=F32
    )


def extended(cells, width, fwd, bwd):
    head = lax.slice_in_dim(cells, 0, width, axis=0)
    tail = lax.slice_in_dim(cells, cells.shape[0] - width, cells.shape[0], axis=0)
    return jnp.concatenate([send(tail, fwd), cells, send(head, bwd)], axis=0)


def generic_device(
    features,
    cotangent,
    depth_kernel,
    depth_bias,
    norm_gain,
    norm_shift,
    up_weight,
    up_bias,
    down_weight,
    layer_scale,
):
    rows_dev, cols, channels = features.shape
    count = lax.axis_size("rows")
    stages = stages_of(count)
    shard = rows_dev * cols
    half_image = IMG_ROWS // 2
    crossing = [
        (i, (i + 1) % count)
        for i in range(count)
        if ((i + 1) * rows_dev - half_image) % IMG_ROWS != 0
    ]
    fwd = crossing
    bwd = [(b, a) for a, b in crossing]
    pieces = 2
    width = channels // pieces

    def gather(value):
        outs = []
        for p in range(pieces):
            part = value[:, p * width : (p + 1) * width]
            for stride, size in stages:
                part = gather_stage(part, count, stride, size)
            outs.append(part.reshape(shard * count, width))
        return outs

    near = extended(features, 3, fwd, bwd).astype(F32)
    cot_scaled = (
        (cotangent.astype(F32) * layer_scale).astype(BF16).reshape(shard, channels)
    )
    cot_all = gather(cot_scaled)
    padded = jnp.pad(near, ((0, 0), (3, 3), (0, 0)))
    conv_out = jnp.zeros((rows_dev, cols, channels), F32)
    for i in range(7):
        for j in range(7):
            conv_out = conv_out + depth_kernel[i, j] * padded[i : i + rows_dev, j : j + cols]
    conv_out = conv_out + depth_bias
    row_mean = jnp.mean(conv_out, axis=-1, keepdims=True)
    centred = conv_out - row_mean
    inv_std = lax.rsqrt(jnp.mean(centred * centred, axis=-1, keepdims=True) + 1e-06)
    unit_norm = centred * inv_std
    normed = (unit_norm * norm_gain + norm_shift).astype(BF16).reshape(shard, channels)
    normed_all = gather(normed)

    hid_grad = sum(
        contract(cot_all[p], down_weight[:, p * width : (p + 1) * width], 1, 1)
        for p in range(pieces)
    )
    pre_act = up_bias + sum(
        contract(normed_all[p], up_weight[p * width : (p + 1) * width], 1, 0)
        for p in range(pieces)
    )
    value, slope = gelu_parts(pre_act)
    hidden = value.astype(BF16)
    act_grad = (hid_grad * slope).astype(BF16)

    norm_parts = []
    for p in range(pieces):
        part = contract(act_grad, up_weight[p * width : (p + 1) * width], 1, 1).astype(BF16)
        lead = [size for _, size in reversed(stages)]
        part = part.reshape(*lead, shard, width)
        for stride, size in reversed(stages):
            part = scatter_stage(part, count, stride, size)
            if stride != stages[0][0]:
                part = part.astype(BF16)
        norm_parts.append(part)
    norm_grad = jnp.concatenate(norm_parts, axis=-1).reshape(rows_dev, cols, channels)

    up_bias_grad = jnp.sum(act_grad.astype(F32), axis=0)
    down_grad = jnp.concatenate([contract(hidden, c, 0, 0) for c in cot_all], axis=1)
    up_grad = jnp.concatenate([contract(n, act_grad, 0, 0) for n in normed_all], axis=0)

    gain_part = jnp.sum(norm_grad * unit_norm, axis=(0, 1))
    shift_part = jnp.sum(norm_grad, axis=(0, 1))
    scaled = norm_grad * norm_gain
    conv_grad = inv_std * (
        scaled
        - jnp.mean(scaled, axis=-1, keepdims=True)
        - unit_norm * jnp.mean(scaled * unit_norm, axis=-1, keepdims=True)
    )
    bias_part = jnp.sum(conv_grad, axis=(0, 1))
    rows_out = [
        jnp.sum(conv_grad * padded[i : i + rows_dev, j : j + cols], axis=(0, 1))
        for i in range(7)
        for j in range(7)
    ]
    near_grad = extended(conv_grad.astype(BF16), 3, fwd, bwd).astype(F32)
    grad_padded = jnp.pad(near_grad, ((0, 0), (3, 3), (0, 0)))

    chips = count // 2
    per = -(-52 // chips)
    small = jnp.stack(rows_out + [gain_part, shift_part, bias_part])
    small = jnp.pad(small, ((0, per * chips - 52), (0, 0)))
    half = channels // 2
    small = small.reshape(chips, per, 2, half).transpose(2, 0, 1, 3)
    core = lax.axis_index("rows") % 2
    swapped = jnp.where(core == 0, small, small[::-1])
    swapped = swapped.astype(BF16)
    mine = swapped[0].astype(F32) + send(
        swapped[1], from_ahead(count, 1, 2, 1)
    ).astype(F32)
    mine = mine.astype(BF16)
    chip = lax.axis_index("rows") // 2
    ahead = jnp.roll(mine, -chip, axis=0)
    total = ahead[0].astype(F32)
    for step in range(1, chips):
        back = [(dst, src) for src, dst in from_ahead(count, 2, chips, step)]
        total = total + send(ahead[step], back).astype(F32)
    total = total.astype(BF16)
    every = [total] + [
        send(total, from_ahead(count, 2, chips, step)) for step in range(1, chips)
    ]
    every = jnp.roll(jnp.stack(every), chip, axis=0)
    other = send(every, from_ahead(count, 1, 2, 1))
    both = jnp.where(
        core == 0,
        jnp.concatenate([every, other], axis=-1),
        jnp.concatenate([other, every], axis=-1),
    )
    both = both.reshape(per * chips, channels).astype(F32)
    kernel_grad = both[:49].reshape(7, 7, channels)
    gain_grad, shift_grad, depth_bias_grad = both[49], both[50], both[51]

    back_term = jnp.zeros((rows_dev, cols, channels), F32)
    for i in range(7):
        for j in range(7):
            back_term = back_term + depth_kernel[i, j] * grad_padded[
                6 - i : 6 - i + rows_dev, 6 - j : 6 - j + cols
            ]
    input_grad = (cotangent.astype(F32) + back_term).astype(BF16)
    return (
        input_grad,
        up_grad,
        up_bias_grad,
        down_grad,
        kernel_grad,
        depth_bias_grad,
        gain_grad,
        shift_grad,
    )


LANES = 128
VMEM = pltpu.VMEM
VSPEC = pl.BlockSpec(memory_space=pltpu.VMEM)
SSPEC = pl.BlockSpec(memory_space=pltpu.SMEM)
EXACT = lax.Precision.HIGHEST
MIB = 1024 * 1024


def z_pairs(step):
    return from_ahead(16, 4, 4, step)


def flipped(pairs):
    return [(dst, src) for src, dst in pairs]


Y_PAIRS = from_ahead(16, 2, 2, 1)
C_PAIRS = from_ahead(16, 1, 2, 1)


def after(value, other):
    return lax.optimization_barrier((value, other))[0]


def gather_chips(shard):
    with jax.named_scope("feat_z"):
        planes = [shard] + [send(shard, z_pairs(step)) for step in (1, 2, 3)]
    with jax.named_scope("feat_y"):
        return planes, [send(plane, Y_PAIRS) for plane in planes]


def lane_tile(tile):
    return pl.ds(pl.multiple_of(tile * LANES, LANES), LANES)


def sixteen(block):
    return pl.ds(pl.multiple_of(block * 16, 16), 16)


def place_and_convolve(idx, pieces, came, kern, bias, feats, conv, turn, total, first_tile):
    z, y, core = idx[0], idx[1], idx[2]
    tiles = feats.shape[0]
    edge = jnp.zeros((tiles, 4, 8, LANES), F32)
    feats[:, :, 0:8, :] = edge
    feats[:, :, 40:48, :] = edge

    def place(piece, row):
        for tile in range(tiles):
            lanes = slice((first_tile + tile) * LANES, (first_tile + tile + 1) * LANES)
            for r in range(4):
                turn[tile % 4, 4 * r : 4 * r + 4, :] = piece[r, :, lanes].astype(F32)
            for col in range(4):
                feats[tile, col, pl.ds(8 + row, 4), :] = turn[
                    tile % 4, pl.ds(col, 4, stride=4), :
                ]

    for yr in range(2):
        for step in range(4):
            at = (z + step + 3) % 4

            @pl.when(at // 2 == core)
            def _():
                place(pieces[4 * yr + step], 16 * (at % 2) + 8 * ((y + yr) % 2) + 4 * core)

        for half in range(2):
            place(came[yr].at[half], 16 * half + 8 * ((y + yr) % 2) + 4 * (1 - core))

    def conv_tile(tile, carry):
        lanes = lane_tile(first_tile + tile)
        for part in range(2):
            acc = [jnp.broadcast_to(bias[0:1, lanes], (16, LANES))] * 4
            for i in range(7):
                for src in range(4):
                    rows = feats[tile, src, pl.ds(5 + 16 * part + i, 16), :]
                    for col in range(4):
                        j = src - col + 3
                        acc[col] = acc[col] + kern[i, j : j + 1, lanes] * rows
            for col in range(4):
                at = pl.ds(64 * part + col, 16, stride=4)
                conv[tile, at, :] = acc[col]
        total[...] = total[...] + conv[tile]
        return carry

    lax.fori_loop(0, tiles, conv_tile, 0)


def conv_kernel(idx, *refs):
    kern, bias, feats, conv, total, turn = refs[10:]
    total[...] = jnp.zeros_like(total)
    place_and_convolve(
        idx, refs[:8], refs[8:10], kern, bias, feats, conv, turn, total, 0
    )


def conv_norm_kernel(idx, *refs):
    kern, bias, gain, shift, feats_low, conv_low, total_low = refs[10:17]
    normed, f_slice, u_slice, inv_slice = refs[17:21]
    feats, conv, turn, total, mean_ref, inv_ref = refs[21:]
    tiles = feats.shape[0]
    channels = 2 * tiles * LANES
    total[...] = total_low[...]
    place_and_convolve(
        idx, refs[:8], refs[8:10], kern, bias, feats, conv, turn, total, tiles
    )
    mean = jnp.sum(total[...], axis=-1, keepdims=True) / channels
    mean_ref[...] = jnp.broadcast_to(mean, mean_ref.shape)
    total[...] = jnp.zeros_like(total)
    halves = ((0, conv_low, feats_low), (tiles, conv, feats))

    def square_tile(tile, carry):
        low, high = conv_low[tile] - mean_ref[...], conv[tile] - mean_ref[...]
        total[...] = total[...] + (low * low + high * high)
        return carry

    lax.fori_loop(0, tiles, square_tile, 0)
    spread = jnp.sum(total[...], axis=-1, keepdims=True) / channels
    inv_ref[...] = jnp.broadcast_to(lax.rsqrt(spread + 1e-06), inv_ref.shape)

    def norm_tile(tile, carry):
        for start, values, _ in halves:
            lanes = lane_tile(start + tile)
            unit = (values[tile] - mean_ref[...]) * inv_ref[...]
            normed[:, lanes] = (unit * gain[0:1, lanes] + shift[0:1, lanes]).astype(BF16)
        return carry

    lax.fori_loop(0, tiles, norm_tile, 0)
    chip = idx[0] * 2 + idx[1]
    inv_slice[...] = inv_ref[...]
    for start, values, padded in halves:

        @pl.when((chip >= 4) == (start > 0))
        def _():
            for k in range(3):
                tile = (chip % 4) * 3 + k
                u_slice[k] = (values[tile] - mean_ref[...]) * inv_ref[...]
                f_slice[k] = padded[tile]


def cot_kernel(idx, *refs):
    layer_scale, cot_all, cot_slice = refs[8:]
    z, y, core = idx[0], idx[1], idx[2]
    chip = z * 2 + y
    own = lane_tile(chip * 3), lane_tile(chip * 3 + 1), lane_tile(chip * 3 + 2)
    for yr in range(2):
        for cr in range(2):
            for step in range(4):
                piece = refs[4 * cr + step].at[yr]
                at = (z + step + 3) % 4
                away = (at // 2 + core) % 2
                block = 4 * (at % 2) + 2 * ((y + yr) % 2) + (core + cr) % 2
                scaled = piece[...].astype(F32) * layer_scale[...]
                cot_all[sixteen(8 * away + block), :] = scaled.astype(BF16)

                @pl.when(away == 0)
                def _():
                    for k in range(3):
                        cot_slice[k, sixteen(block), :] = piece[:, own[k]].astype(F32)


def fold_kernel(gain, shift, weight, kern, shard, gain_dot, shift_dot, kern_out, shard_out):
    kern_out[...] = kern[...]
    shard_out[...] = shard[...]
    place = lax.broadcasted_iota(jnp.int32, (16, gain.shape[1]), 0)
    scale, offset = gain[...], shift[...]
    scale_hi = scale.astype(BF16).astype(F32)
    offset_hi = offset.astype(BF16).astype(F32)
    both = jnp.where(place == 0, scale_hi, 0.0)
    both = jnp.where(place == 1, scale - scale_hi, both)
    both = jnp.where(place == 2, offset_hi, both)
    both = jnp.where(place == 3, offset - offset_hi, both)
    product = jnp.dot(both.astype(BF16), weight[...], preferred_element_type=F32)
    gain_dot[...] = jnp.broadcast_to(product[0:1] + product[1:2], gain_dot.shape)
    shift_dot[...] = jnp.broadcast_to(product[2:3] + product[3:4], shift_dot.shape)


def up_kernel(normed, weight, up_bias, shift_dot, hidden, slope, centred):
    tile = 256
    for start in range(0, hidden.shape[1], tile):
        at = slice(start, start + tile)
        plain = jnp.dot(normed[...], weight[:, at], preferred_element_type=F32)
        pre_act = plain + up_bias[0:1, at]
        cdf = 0.5 * (1.0 + lax.erf(pre_act * 0.7071067811865476))
        hidden[:, at] = (pre_act * cdf).astype(BF16)
        slope[:, at] = cdf + pre_act * jnp.exp(-0.5 * pre_act * pre_act) * 0.3989422804014327
        centred[:, at] = plain - shift_dot[0:1, at]


def act_kernel(
    cot_all, weight, gain_dot, slope_own, slope_other, centred_own, centred_other,
    act_own, act_other, bias_grad, sums_own, sums_other,
):
    tile = 256
    halves = (
        (0, slope_own, centred_own, act_own, sums_own),
        (128, slope_other, centred_other, act_other, sums_other),
    )
    parts = [jnp.zeros((128, LANES), F32) for _ in range(4)]
    for start in range(0, act_own.shape[1], tile):
        at = slice(start, start + tile)
        hid_grad = contract(cot_all[...], weight[at, :], 1, 1)
        column = jnp.zeros((1, tile), F32)
        for half, (row, slope, centred, act_grad, _) in enumerate(halves):
            act = (hid_grad[row : row + 128] * slope[:, at]).astype(BF16)
            act_grad[:, at] = act
            act = act.astype(F32)
            column = column + jnp.sum(act, axis=0, keepdims=True)
            by_gain = act * gain_dot[0:1, at]
            by_unit = act * centred[:, at]
            for lane in range(0, tile, LANES):
                parts[2 * half] = parts[2 * half] + by_gain[:, lane : lane + LANES]
                parts[2 * half + 1] = parts[2 * half + 1] + by_unit[:, lane : lane + LANES]
        bias_grad[0:1, at] = column
    ones = jnp.ones((8, LANES), F32)
    for half, (_, _, _, _, sums) in enumerate(halves):
        for which in range(2):
            sums[8 * which : 8 * which + 8, :] = lax.dot_general(
                ones, parts[2 * half + which], (((1,), (1,)), ((), ())),
                precision=EXACT, preferred_element_type=F32,
            )


def norm_grad_kernel(steps, idx, act_own, act_other, weight, sums_own, sums_other, keep, away):
    both = jnp.concatenate([act_other[...], act_own[...]], axis=0)
    for at, step in enumerate(steps):
        for yr in range(2):
            chip = 2 * ((idx[0] + step) % 4) + (idx[1] + yr) % 2
            rows = weight[pl.ds(pl.multiple_of(chip * 384, 128), 384), :]
            product = contract(both, rows, 1, 1)
            for ref, part, sums in ((away, 0, sums_other), (keep, 128, sums_own)):
                ref[at, yr, 0:128, :] = product[part : part + 128].astype(ref.dtype)
                ref[at, yr, 128:144, 0:128] = sums[...].astype(ref.dtype)
                ref[at, yr, 128:144, 128:384] = jnp.zeros((16, 256), ref.dtype)


def grad_kernel(left_own, left_other, right_own, right_other, *rest):
    left = jnp.concatenate([left_own[...], left_other[...]], axis=0).T
    right = jnp.concatenate([right_own[...], right_other[...]], axis=0)
    rest[-1][...] = contract(left, right, 1, 0)


def conv_back_kernel(
    idx, own, near_1, near_2, near_3, f_slice, u_slice, inv_slice, gain, kern, cot_slice,
    ig_keep, core_msg, small_keep, cg, turn, back, small,
):
    chip, y, core = idx[0] * 2 + idx[1], idx[1], idx[2]
    channels = gain.shape[1]

    def summed(rows, lanes):
        return (
            own[rows, lanes]
            + near_1[rows, lanes].astype(F32)
            + near_2[rows, lanes].astype(F32)
            + near_3[rows, lanes].astype(F32)
        )

    sums = summed(slice(128, 144), slice(0, 128))
    place = lax.broadcasted_iota(jnp.int32, (16, LANES), 0)

    def per_token(row):
        pick = jnp.where(place == row, 1.0 / channels, 0.0).astype(F32)
        return lax.dot_general(
            sums, pick, (((0,), (0,)), ((), ())), precision=EXACT, preferred_element_type=F32
        )

    mean_1, mean_2 = per_token(0), per_token(8)
    cg[:, :, 0:8, :] = jnp.zeros((3, 4, 8, LANES), F32)
    cg[:, :, 40:48, :] = jnp.zeros((3, 4, 8, LANES), F32)
    small[...] = jnp.zeros_like(small)
    for k in range(3):
        lanes = slice(k * LANES, (k + 1) * LANES)
        wide = lane_tile(chip * 3 + k)
        norm_grad = summed(slice(0, 128), lanes)
        unit = u_slice[k]
        scaled = norm_grad * gain[0:1, wide]
        grad = inv_slice[...] * (scaled - mean_1 - unit * mean_2)
        turn[k] = grad
        for col in range(4):
            cg[k, col, 8:40, :] = turn[k, pl.ds(col, 32, stride=4), :]
        small[56:57, lanes] = jnp.sum(norm_grad * unit, axis=0, keepdims=True)
        small[57:58, lanes] = jnp.sum(norm_grad, axis=0, keepdims=True)
        small[58:59, lanes] = jnp.sum(grad, axis=0, keepdims=True)
        for i in range(7):
            acc = [None] * 7
            for src in range(4):
                rows = f_slice[k, src, 5 + i : 37 + i, :]
                for col in range(4):
                    j = src - col + 3
                    term = cg[k, col, 8:40, :] * rows
                    acc[j] = term if acc[j] is None else acc[j] + term
            for j in range(7):
                small[8 * i + j : 8 * i + j + 1, lanes] = jnp.sum(acc[j], axis=0, keepdims=True)
        for part in range(2):
            acc = [cot_slice[k, pl.ds(64 * part + col, 16, stride=4), :] for col in range(4)]
            for i in range(7):
                for src in range(4):
                    start = 11 + 16 * part - i
                    rows = cg[k, src, start : start + 16, :]
                    for col in range(4):
                        j = col - src + 3
                        acc[col] = acc[col] + kern[i, j : j + 1, wide] * rows
            for col in range(4):
                back[k, pl.ds(64 * part + col, 16, stride=4), :] = acc[col]
        for half in range(2):
            for yr in range(2):
                for cr in range(2):
                    block = 4 * half + 2 * ((y + yr) % 2) + (core + cr) % 2
                    ref = core_msg if cr else ig_keep
                    ref[2 * half + yr, :, lanes] = back[k, sixteen(block), :].astype(BF16)
    for part in range(2):
        core_msg[4 + part] = small[sixteen(2 * (1 - core) + part), :].astype(BF16)
        small_keep[part] = small[sixteen(2 * core + part), :]


def route_kernel(idx, ig_keep, core_msg, small_keep, *msgs):
    z, core = idx[0], idx[2]
    total = [
        (small_keep[part] + core_msg[4 + part].astype(F32)).astype(BF16) for part in range(2)
    ]
    for step in range(4):
        at = (z + step + 3) % 4
        image, half = at // 2, at % 2
        for yr in range(2):
            kept, came = ig_keep[2 * half + yr], core_msg[2 * half + yr]
            msgs[step][yr] = jnp.where(image == core, kept, came)
        for part in range(2):
            msgs[step][2 + part] = total[part]


def place_kernel(idx, *refs):
    msgs, came, across_core = refs[:4], refs[4], refs[5]
    tokens, kernel_grad, gain_grad, shift_grad, bias_grad = refs[6:]
    z, y, core = idx[0], idx[1], idx[2]
    for step in range(4):
        plane = (z + 4 - step) % 4
        for yr in range(2):
            chip = plane * 2 + (y + yr) % 2
            lanes = pl.ds(pl.multiple_of(chip * 384, 128), 384)
            block = (came[step, 0] if yr else msgs[step][0]).astype(F32)
            for row in range(4):
                tokens[row, :, lanes] = block[4 * row : 4 * row + 4].astype(BF16)
            for part in range(2):
                mine = (came[step, 1 + part] if yr else msgs[step][2 + part]).astype(F32)
                other = across_core[yr, step, part].astype(F32)
                low = jnp.where(core == 0, mine, other)
                high = jnp.where(core == 0, other, mine)
                for sub in range(2):
                    at = 2 * part + sub
                    rows = slice(8 * sub, 8 * sub + 7)
                    kernel_grad[at, :, lanes] = low[rows]
                    if at < 3:
                        kernel_grad[4 + at, :, lanes] = high[rows]
                    else:
                        gain_grad[0:1, lanes] = high[8:9]
                        shift_grad[0:1, lanes] = high[9:10]
                        bias_grad[0:1, lanes] = high[10:11]


def shape(dims, dtype):
    return jax.ShapeDtypeStruct(dims, dtype)


def call(kernel, micros, room, out_shape, inputs, scratch=(), scalars=1):
    return pl.pallas_call(
        kernel,
        out_shape=out_shape,
        in_specs=[SSPEC] * scalars + [VSPEC] * (len(inputs) - scalars),
        out_specs=jax.tree.map(lambda _: VSPEC, out_shape),
        scratch_shapes=list(scratch),
        compiler_params=pltpu.CompilerParams(vmem_limit_bytes=room * MIB),
        cost_estimate=cost(micros),
    )(*inputs)


def cost(micros):
    return pl.CostEstimate(
        flops=int(micros * 1.1e9), bytes_accessed=int(micros * 3.4e6), transcendentals=0
    )


def half_gradient(part, left, right, tile, so_far=None):
    rows, cols = left[0].shape[1], right[0].shape[1]
    steps = rows // 2 // tile
    left_spec = pl.BlockSpec((128, tile), lambda m: (0, part * steps + m))
    right_spec = pl.BlockSpec((128, cols), lambda m: (0, 0))
    whole = right[1] is right[0]
    other_spec = pl.BlockSpec((128, cols), lambda m: (1, 0)) if whole else right_spec
    extra = () if so_far is None else (so_far,)
    return pl.pallas_call(
        grad_kernel,
        grid=(steps,),
        out_shape=shape((rows, cols), F32),
        in_specs=[left_spec, left_spec, right_spec, other_spec]
        + [pl.BlockSpec(memory_space=pl.ANY)] * len(extra),
        out_specs=pl.BlockSpec((tile, cols), lambda m: (part * steps + m, 0)),
        input_output_aliases={4: 0} if extra else {},
        compiler_params=pltpu.CompilerParams(vmem_limit_bytes=16 * MIB),
        cost_estimate=cost(2.5),
    )(*left, *right, *extra)


def sliced_device(
    features,
    cotangent,
    depth_kernel,
    depth_bias,
    norm_gain,
    norm_shift,
    up_weight,
    up_bias,
    down_weight,
    layer_scale,
):
    channels, hidden_dev = up_weight.shape
    tiles = channels // LANES
    index = lax.axis_index("rows")
    z, y, core = index // 4, (index // 2) % 2, index % 2
    idx = jnp.stack([z, y, core]).astype(jnp.int32)
    bias_row, gain_row = depth_bias.reshape(1, channels), norm_gain.reshape(1, channels)
    shift_row, scale_row = norm_shift.reshape(1, channels), layer_scale.reshape(1, channels)
    up_bias_row = up_bias.reshape(1, hidden_dev)

    cot_shard = cotangent.reshape(16, channels)
    planes, across = gather_chips(features)
    gain_dot, shift_dot, kern, own_shard = call(
        fold_kernel,
        1.5,
        10,
        (
            shape((8, hidden_dev), F32),
            shape((8, hidden_dev), F32),
            shape(depth_kernel.shape, F32),
            shape(features.shape, BF16),
        ),
        (gain_row, shift_row, up_weight, depth_kernel, features),
        scalars=0,
    )
    planes = [own_shard] + planes[1:]
    picks = [(2 * (1 - core) + half + 1 - z) % 4 for half in range(2)]
    chosen = [
        jnp.stack([lax.select_n(pick, *pieces) for pick in picks]) for pieces in (planes, across)
    ]
    with jax.named_scope("feat_core"):
        feat_came = [send(pieces, C_PAIRS) for pieces in chosen]
    with jax.named_scope("cot_y"):
        cot_pair = jnp.stack([cot_shard, send(cot_shard, Y_PAIRS)])
    with jax.named_scope("cot_z"):
        cot_late = after(cot_pair, tuple(planes[1:]))
        ahead, behind = send(cot_late, z_pairs(1)), send(cot_late, z_pairs(3))
        cot_planes = [cot_pair, ahead, send(ahead, z_pairs(1)), behind]
    half_tiles = tiles // 2
    turn = VMEM((4, 16, LANES), F32)
    square = VMEM((128, LANES), F32)
    conv_args = (*planes, *across, *feat_came, kern, bias_row)
    feats_low, conv_low, total_low = call(
        conv_kernel,
        8.0,
        12,
        (
            shape((half_tiles, 4, 48, LANES), F32),
            shape((half_tiles, 128, LANES), F32),
            shape((128, LANES), F32),
        ),
        (after(idx, (cot_planes[1], cot_planes[3])), *conv_args),
        (turn,),
    )
    normed, f_slice, u_slice, inv_slice = call(
        conv_norm_kernel,
        8.0,
        12,
        (
            shape((128, channels), BF16),
            shape((3, 4, 48, LANES), F32),
            shape((3, 128, LANES), F32),
            shape((128, LANES), F32),
        ),
        (
            idx, *conv_args, gain_row, shift_row,
            feats_low, conv_low, total_low,
        ),
        (
            VMEM((half_tiles, 4, 48, LANES), F32),
            VMEM((half_tiles, 128, LANES), F32),
            turn,
            square,
            square,
            square,
        ),
    )
    with jax.named_scope("cot_core"):
        cot_came = [send(after(plane, inv_slice), C_PAIRS) for plane in cot_planes]
    normed_other = send(after(normed, cot_planes[2]), C_PAIRS)
    half_f32 = shape((128, hidden_dev), F32)
    half_bf16 = shape((128, hidden_dev), BF16)
    ups = [
        call(
            up_kernel,
            0.1,
            12,
            (half_bf16, half_f32, half_f32),
            (value, up_weight, up_bias_row, shift_dot),
            scalars=0,
        )
        for value in (normed, normed_other)
    ]
    hidden, slope, centred = zip(*ups)
    cot_all, cot_slice = call(
        cot_kernel,
        1.5,
        8,
        (shape((256, channels), BF16), shape((3, 128, LANES), F32)),
        (after(idx, slope), *cot_planes, *cot_came, scale_row),
    )
    act_own, act_other, up_bias_grad, *sums = call(
        act_kernel,
        2.2,
        12,
        (
            half_bf16,
            half_bf16,
            shape((1, hidden_dev), F32),
            shape((16, LANES), F32),
            shape((16, LANES), F32),
        ),
        (cot_all, down_weight, gain_dot, *slope, *centred),
        scalars=0,
    )
    act_grad = (act_own, act_other)

    arrived, came_at, keep_at, across_at = {}, {}, {}, {}
    for pair in ((2, 3), (1, 0)):
        keep, away = call(
            functools.partial(norm_grad_kernel, pair),
            1.6,
            10,
            (shape((2, 2, 144, 384), F32), shape((2, 2, 144, 384), BF16)),
            (idx, *act_grad, up_weight, *sums),
        )
        came = send(away, C_PAIRS)
        for at, step in enumerate(pair):
            came_at[step], keep_at[step] = came[at].astype(F32), keep[at]
            across_at[step] = send((keep[at, 1] + came_at[step][1]).astype(BF16), Y_PAIRS)
    cots = (cot_all, cot_all)
    down_low = half_gradient(0, after(hidden, came), cots, 128)
    for step in (2, 3, 1, 0):
        total = keep_at[step][0] + came_at[step][0]
        if step == 1:
            total, down_low = lax.optimization_barrier((total, down_low))
        total = total + across_at[step].astype(F32)
        if step:
            total = send(total.astype(BF16), flipped(z_pairs(step)))
        arrived[step] = total
    down_grad = half_gradient(1, after(hidden, across_at[0]), cots, 128, down_low)
    late_idx, down_grad = lax.optimization_barrier((idx, down_grad))
    ig_keep, core_msg, small_keep = call(
        conv_back_kernel,
        2.2,
        12,
        (shape((4, 16, 384), BF16), shape((6, 16, 384), BF16), shape((2, 16, 384), F32)),
        (
            late_idx, arrived[0], arrived[1], arrived[2], arrived[3], f_slice, u_slice, inv_slice,
            gain_row, kern, cot_slice,
        ),
        (
            VMEM((3, 4, 48, LANES), F32),
            VMEM((3, 128, LANES), F32),
            VMEM((3, 128, LANES), F32),
            VMEM((64, 384), F32),
        ),
    )
    core_msg = send(core_msg, C_PAIRS)
    msgs = call(
        route_kernel,
        0.5,
        4,
        tuple(shape((4, 16, 384), BF16) for _ in range(4)),
        (idx, ig_keep, core_msg, small_keep),
    )
    msgs = [msgs[0]] + [send(msgs[step], flipped(z_pairs(step))) for step in (1, 2, 3)]
    came_near = send(msgs[0][1:4], Y_PAIRS)
    up_low = half_gradient(0, after((normed, normed_other), msgs[3]), act_grad, 512)
    msgs, up_low = lax.optimization_barrier((msgs, up_low))
    came_far = send(jnp.stack([msg[1:4] for msg in msgs[1:]]), Y_PAIRS)
    came = jnp.concatenate([came_near[None], came_far])
    up_grad = half_gradient(1, after((normed, normed_other), msgs[1]), act_grad, 512, up_low)
    near = jnp.stack([msg[2:4] for msg in msgs])
    both, up_grad = lax.optimization_barrier((jnp.stack([near, came[:, 1:3]]), up_grad))
    across_core = send(both, C_PAIRS)
    row = shape((1, channels), F32)
    tokens, kernel_grad, gain_grad, shift_grad, depth_bias_grad = call(
        place_kernel,
        0.8,
        8,
        (shape((4, 4, channels), BF16), shape((7, 7, channels), F32), row, row, row),
        (idx, *msgs, came, across_core),
    )
    return (
        tokens,
        up_grad,
        up_bias_grad.reshape(hidden_dev),
        down_grad,
        kernel_grad,
        depth_bias_grad.reshape(channels),
        gain_grad.reshape(channels),
        shift_grad.reshape(channels),
    )


def on_device(features, *rest):
    rows_dev, cols, channels = features.shape
    fits = lax.axis_size("rows") == 16 and rows_dev == 4 and cols == 4 and channels == 3072
    return (sliced_device if fits else generic_device)(features, *rest)


def solution(mesh):
    in_specs = (
        P(("groups", "rows"), None, None),
        P(("groups", "rows"), None, None),
        P(),
        P(),
        P(),
        P(),
        P(None, "rows"),
        P("rows"),
        P("rows", None),
        P(),
    )
    out_specs = (
        P(("groups", "rows"), None, None),
        P("groups", "rows"),
        P(("groups", "rows")),
        P(("groups", "rows"), None),
        P("groups", None, None),
        P("groups"),
        P("groups"),
        P("groups"),
    )
    return jax.shard_map(
        on_device, mesh=mesh, in_specs=in_specs, out_specs=out_specs, check_vma=False
    )
```
